256 devices in a mesh: seq: 64 (over x, z, core), vocab: 4 (over y).
Axes of the slice: x: 4, y: 4, z: 8, core: 2. Of those that a mesh axis runs over, the one named last changes fastest.
Arguments:
- query: bfloat16 [8192, 64, 576], P('seq', 'vocab'), may hold values from -150 to 150
- latent_cache: bfloat16 [512, 64, 576], P('seq'), may hold values from -4 to 4
- block_lists: int32 [512, 16], P('seq'), may hold values from -1 to 511, as said below
- d_out: bfloat16 [8192, 64, 512], P('seq', 'vocab'), may hold values from -3 to 3
Outputs:
- grad_query: bfloat16 [8192, 64, 576], P('seq', 'vocab')
- grad_cache: float32 [512, 64, 576], P('seq', 'vocab')
The draws below stay inside these ranges and needn't reach their ends.
Inputs may be any that keep to these rules, and one draw needn't show every extreme that they name: `block_lists`: list j serves query rows j * 16 to j * 16 + 15. Its first entry is the block that holds those rows; the others are distinct blocks before it, followed by -1 entries that select nothing. The lists of one device's 128 rows name at most 2 distinct blocks held by any one other device, and exactly 2 held by some device, on every device but the first.
All inputs are finite; a program needn't handle non-finite values.
Results may differ from the reference program's by a relative error of at most 0.006.
Values may be sent and summed in bfloat16 or wider, within the bound.
No kernel may reach another device: no remote copies, remote signals or barrier semaphores. Data moves between devices by JAX's collectives and lax.ppermute only.
A program may use at most 192 MiB of HBM per device.

```python
import jax
import jax.numpy as jnp
from jax import lax

VALUE = 512
BLOCK = 64
SEL = 16
QGROUP = 16
CAP = 2
KEYS_DEV = 512
ROWS_DEV = 128
LATENT = 576
HEADS = 64
TOKENS = 8192
CTX = 32768
NBLK = 512


def draw_latent_cache(key, part):
    key = jax.random.fold_in(key, 2)
    flat = jnp.clip(jax.random.normal(key, (CTX, LATENT), jnp.float32), -4.0, 4.0)
    return flat.reshape(NBLK, BLOCK, LATENT).astype(jnp.bfloat16)


def draw_query(key, part):
    key = jax.random.fold_in(key, 3)
    values = jnp.clip(jax.random.normal(key, (TOKENS, HEADS, LATENT), jnp.float32), -4.0, 4.0)
    return values.astype(jnp.bfloat16)


def draw_block_lists(key, part):
    key = jax.random.fold_in(key, 11)
    pool_key, order_key = jax.random.split(key)
    shards = TOKENS // ROWS_DEV
    per_shard = KEYS_DEV // BLOCK
    groups = ROWS_DEV // QGROUP
    inner = jnp.arange(per_shard, dtype=jnp.int32)
    pool_scores = jax.random.randint(pool_key, (shards, shards, per_shard), 0, 1 << 16) * per_shard + inner
    pool_scores = jnp.where(inner[None, None, :] == 0, -1, pool_scores)
    pool = lax.top_k(pool_scores, CAP)[1].astype(jnp.int32)
    owners = jnp.arange(shards, dtype=jnp.int32)
    pooled = (owners[None, :, None] * per_shard + pool).reshape(shards, shards * CAP)
    local = owners[:, None] * per_shard + inner[None, :]
    candidates = jnp.concatenate([local, pooled], axis=1)
    count = per_shard + shards * CAP
    own_in = (KEYS_DEV - ROWS_DEV + jnp.arange(groups, dtype=jnp.int32) * QGROUP) // BLOCK
    slot = jnp.arange(count, dtype=jnp.int32)
    slot_owner = jnp.where(slot < per_shard, -1, (slot - per_shard) // CAP)
    local_ok = (slot[None, None, :] < per_shard) & (slot[None, None, :] < own_in[None, :, None])
    pool_ok = (slot_owner[None, None, :] >= 0) & (slot_owner[None, None, :] < owners[:, None, None])
    usable = local_ok | pool_ok
    group_ids = jnp.arange(groups, dtype=jnp.int32)[None, :, None]
    forced = (group_ids == 0) & (slot_owner[None, None, :] >= 0) & (slot_owner[None, None, :] == owners[:, None, None] - 1)
    forced_first = (group_ids == 1) & (slot_owner[None, None, :] == 0) & (owners[:, None, None] >= 1)
    order = jax.random.randint(order_key, (shards, groups, count), 0, 1 << 16) * count + slot[None, None, :]
    order = jnp.where(forced | forced_first, order + (1 << 16) * count, order)
    order = jnp.where(usable, order, -1 - slot[None, None, :])
    best, picked = lax.top_k(order, SEL - 1)
    spread = jnp.broadcast_to(candidates[:, None, :], (shards, groups, count))
    chosen = jnp.take_along_axis(spread, picked, axis=2)
    chosen = jnp.where(best >= 0, chosen, -1)
    own = owners[:, None] * per_shard + own_in[None, :]
    lists = jnp.concatenate([own[:, :, None], chosen], axis=2)
    return lists.reshape(shards * groups, SEL).astype(jnp.int32)


def steps_of(key, dims, cuts, least, top_value):
    gain = 1.0
    for dim, shards_of in cuts:
        draws = jax.random.uniform(jax.random.fold_in(jax.random.fold_in(key, 6), dim), (shards_of,), jnp.float32, least / len(cuts), top_value / len(cuts))
        gain = gain * jnp.repeat(jnp.exp(draws), dims[dim] // shards_of).reshape((-1,) + (1,) * (len(dims) - 1 - dim))
    return gain


def scatter_about(own_key, shape, scale, reach, cuts=(), kind=jnp.bfloat16):
    result = scale * jax.random.normal(own_key, shape, jnp.float32)
    if cuts:
        result = result * steps_of(own_key, shape, cuts, -0.22, 0.18)
    return jnp.clip(result, -reach, reach).astype(kind)


def setup_inputs(seed: int = 0) -> dict:
    seeds = jax.random.split(jax.random.key(seed), 5)
    query = draw_query(jax.random.fold_in(seeds[4], 71), 0)
    latent_cache = draw_latent_cache(jax.random.fold_in(seeds[4], 71), 0)
    block_lists = draw_block_lists(jax.random.fold_in(seeds[4], 71), 0)
    d_out = scatter_about(seeds[3], (TOKENS, HEADS, VALUE), 0.5, 3.0, ((0, 64), (1, 4)))
    return {"query": query, "latent_cache": latent_cache, "block_lists": block_lists, "d_out": d_out}


score_scale = 0.07216878364870323


def lower(values):
    return lax.optimization_barrier(values.astype(jnp.bfloat16)).astype(jnp.float32)


def attend_local_shard(query, blocks, d_out, latent_cache, shard):
    groups = blocks.shape[0]
    queries = query.reshape(groups, QGROUP, HEADS, LATENT).astype(jnp.float32)
    outs = d_out.reshape(groups, QGROUP, HEADS, VALUE).astype(jnp.float32)
    safe = jnp.maximum(blocks, 0).astype(jnp.int32)
    key_rows = latent_cache[safe].astype(jnp.float32)
    scores = jnp.einsum('grhl,gskl->grhsk', queries, key_rows) * score_scale
    grad_probs = jnp.einsum('grhv,gskv->grhsk', outs, key_rows[..., :VALUE])
    key_pos = blocks[:, :, None] * BLOCK + jnp.arange(BLOCK, dtype=jnp.int32)[None, None, :]
    query_pos = shard * KEYS_DEV + KEYS_DEV - ROWS_DEV + jnp.arange(groups * QGROUP, dtype=jnp.int32).reshape(groups, QGROUP)
    allowed = (blocks[:, None, :, None] >= 0) & (key_pos[:, None, :, :] <= query_pos[:, :, None, None])
    allowed = allowed[:, :, None, :, :]
    masked = jnp.where(allowed, scores, -jnp.inf)
    top = jnp.max(masked, axis=(3, 4), keepdims=True)
    expo = jnp.exp(masked - top)
    probs = expo / jnp.sum(expo, axis=(3, 4), keepdims=True)
    delta = jnp.sum(probs * grad_probs, axis=(3, 4), keepdims=True)
    probability_lower = lower(probs)
    grad_low = lower(score_scale * probs * (grad_probs - delta))
    grad_query = jnp.einsum('grhsk,gskl->grhl', grad_low, key_rows).astype(jnp.bfloat16)
    grad_keys = jnp.einsum('grhsk,grhl->gskl', grad_low, queries)
    grad_values = jnp.einsum('grhsk,grhv->gskv', probability_lower, outs)
    grad_keys = grad_keys + jnp.pad(grad_values, ((0, 0), (0, 0), (0, 0), (0, LATENT - VALUE)))
    return grad_query.reshape(groups * QGROUP, HEADS, LATENT), safe, grad_keys


def reference(query, latent_cache, block_lists, d_out):
    shards = TOKENS // ROWS_DEV
    lists_per = ROWS_DEV // QGROUP

    def one_shard(grad_cache, shard):
        start = (shard * ROWS_DEV).astype(jnp.int32)
        queries = lax.dynamic_slice_in_dim(query, start, ROWS_DEV, 0)
        outs = lax.dynamic_slice_in_dim(d_out, start, ROWS_DEV, 0)
        blocks = lax.dynamic_slice_in_dim(block_lists, (shard * lists_per).astype(jnp.int32), lists_per, 0)
        grad_query, safe, grad_keys = attend_local_shard(queries, blocks, outs, latent_cache, shard)
        grad_cache = grad_cache.at[safe.reshape(-1)].add(grad_keys.reshape(-1, BLOCK, LATENT))
        return grad_cache, grad_query

    grad_cache, pieces = lax.scan(one_shard, jnp.zeros((NBLK, BLOCK, LATENT), jnp.float32), jnp.arange(shards, dtype=jnp.int32))
    grad_query = pieces.reshape(TOKENS, HEADS, LATENT)
    return (grad_query, grad_cache)
```

```python
import functools

import jax
import jax.numpy as jnp
from jax import lax
from jax.experimental import pallas as pl
from jax.experimental.pallas import tpu as pltpu
from jax.sharding import PartitionSpec as P

CAP = 2
SCALE = 0.07216878364870323
LOG2E = 1.4426950408889634


def attention_kernel(start_ref, first_ref, q_ref, d_ref, k_ref, gq_ref, gk_ref, acc_ref):
    group = pl.program_id(0)
    tile = pl.program_id(1)
    parts, entries, part_len, latent = k_ref.shape
    keys_n = parts * entries * part_len
    rows, heads = q_ref.shape[1], q_ref.shape[2]
    cols = rows * heads
    value = d_ref.shape[3]
    q = q_ref[0].reshape(cols, latent)
    d = d_ref[0].reshape(cols, value)
    keys = k_ref[...].reshape(keys_n, latent)
    nt = (((1,), (1,)), ((), ()))
    scores = lax.dot_general(keys, q, nt, preferred_element_type=jnp.float32)
    grad_probs = lax.dot_general(keys[:, :value], d, nt, preferred_element_type=jnp.float32)

    shape = (part_len, cols)
    row = lax.broadcasted_iota(jnp.int32, shape, 1) // heads
    limit = first_ref[0] + group * rows + row - lax.broadcasted_iota(jnp.int32, shape, 0)
    strips = []
    for i in range(parts * entries):
        strip = scores[i * part_len : (i + 1) * part_len]
        strips.append(jnp.where(start_ref[group, i] <= limit, strip, -jnp.inf))
    masked = jnp.concatenate(strips, axis=0)
    top = jnp.max(masked, axis=0, keepdims=True)
    expo = jnp.exp2((masked - top) * (SCALE * LOG2E))
    inverse = 1.0 / jnp.sum(expo, axis=0, keepdims=True)
    delta = jnp.sum(expo * grad_probs, axis=0, keepdims=True) * inverse
    probs_low = (expo * inverse).astype(jnp.bfloat16)
    grad_low = (expo * (inverse * SCALE) * (grad_probs - delta)).astype(jnp.bfloat16)

    gq = lax.dot_general(grad_low, keys, (((0,), (0,)), ((), ())), preferred_element_type=jnp.float32)
    gq_ref[0] = gq.astype(jnp.bfloat16).reshape(rows, heads, latent)
    gk = jnp.dot(grad_low, q, preferred_element_type=jnp.float32)
    gv = jnp.dot(probs_low, d, preferred_element_type=jnp.float32)

    @pl.when(tile == 0)
    def _():
        acc_ref[...] = gk
        acc_ref[:, :value] += gv

    @pl.when(tile > 0)
    def _():
        acc_ref[...] += gk
        acc_ref[:, :value] += gv

    @pl.when(tile == pl.num_programs(1) - 1)
    def _():
        gk_ref[...] = acc_ref[...].astype(jnp.bfloat16).reshape(gk_ref.shape)


def attention(start, first, q, d, keys, groups):
    members, rows_all, heads, latent = q.shape
    value = d.shape[3]
    rows = rows_all // groups
    parts, entries_all, part_len, _ = keys.shape
    entries = entries_all // groups
    flops = 2 * members * rows_all * heads * parts * entries * part_len * (3 * latent + 2 * value)
    return pl.pallas_call(
        attention_kernel,
        grid_spec=pltpu.PrefetchScalarGridSpec(
            num_scalar_prefetch=2,
            grid=(groups, members),
            in_specs=[
                pl.BlockSpec((1, rows, heads, latent), lambda g, t, *_: (t, g, 0, 0)),
                pl.BlockSpec((1, rows, heads, value), lambda g, t, *_: (t, g, 0, 0)),
                pl.BlockSpec((parts, entries, part_len, latent), lambda g, t, *_: (0, g, 0, 0)),
            ],
            out_specs=[
                pl.BlockSpec((1, rows, heads, latent), lambda g, t, *_: (t, g, 0, 0)),
                pl.BlockSpec((parts, entries, part_len, latent), lambda g, t, *_: (0, g, 0, 0)),
            ],
            scratch_shapes=[pltpu.VMEM((parts * entries * part_len, latent), jnp.float32)],
        ),
        out_shape=[
            jax.ShapeDtypeStruct(q.shape, jnp.bfloat16),
            jax.ShapeDtypeStruct(keys.shape, jnp.bfloat16),
        ],
        compiler_params=pltpu.CompilerParams(
            dimension_semantics=("arbitrary", "arbitrary"), vmem_limit_bytes=50 * 1024 * 1024
        ),
        cost_estimate=pl.CostEstimate(flops=flops, bytes_accessed=16 << 20, transcendentals=1 << 21),
    )(start, first, q, d, keys)


def sum_by_block_kernel(index_ref, in_ref, local_ref, slots_ref, table_ref):
    table_ref[...] = jnp.zeros_like(table_ref)

    def add(i, carry):
        table_ref[index_ref[i]] += in_ref[i].astype(jnp.float32)
        return carry

    lax.fori_loop(0, in_ref.shape[0], add, 0)
    per = local_ref.shape[0]
    local_ref[...] = table_ref[:per]
    slots_ref[...] = table_ref[per:].astype(jnp.bfloat16)


def sum_by_block(index, entries, per_shard, slots):
    _, part_len, latent = entries.shape
    return pl.pallas_call(
        sum_by_block_kernel,
        in_specs=[pl.BlockSpec(memory_space=pltpu.SMEM), pl.BlockSpec(memory_space=pltpu.VMEM)],
        out_specs=[pl.BlockSpec(memory_space=pltpu.VMEM)] * 2,
        out_shape=[
            jax.ShapeDtypeStruct((per_shard, part_len, latent), jnp.float32),
            jax.ShapeDtypeStruct((slots, part_len, latent), jnp.bfloat16),
        ],
        scratch_shapes=[pltpu.VMEM((per_shard + slots, part_len, latent), jnp.float32)],
        compiler_params=pltpu.CompilerParams(vmem_limit_bytes=40 * 1024 * 1024),
        cost_estimate=pl.CostEstimate(flops=2 << 20, bytes_accessed=6 << 20, transcendentals=0),
    )(index, entries)


def receive_kernel(index_ref, in_ref, local_ref, out_ref, table_ref):
    per = local_ref.shape[0]
    table_ref[:per] = local_ref[...]

    def add(i, carry):
        table_ref[index_ref[i]] += in_ref[i].astype(jnp.float32)
        return carry

    lax.fori_loop(0, in_ref.shape[0], add, 0)
    out_ref[...] = table_ref[:per]


def receive(index, arrived, local):
    per, part_len, latent = local.shape
    return pl.pallas_call(
        receive_kernel,
        in_specs=[
            pl.BlockSpec(memory_space=pltpu.SMEM),
            pl.BlockSpec(memory_space=pltpu.VMEM),
            pl.BlockSpec(memory_space=pltpu.VMEM),
        ],
        out_specs=pl.BlockSpec(memory_space=pltpu.VMEM),
        out_shape=jax.ShapeDtypeStruct(local.shape, jnp.float32),
        scratch_shapes=[pltpu.VMEM((per + 1, part_len, latent), jnp.float32)],
        compiler_params=pltpu.CompilerParams(vmem_limit_bytes=40 * 1024 * 1024),
        cost_estimate=pl.CostEstimate(flops=2 << 20, bytes_accessed=4 << 20, transcendentals=0),
    )(index, arrived, local)


def body(query, latent_cache, block_lists, d_out):
    shard = lax.axis_index("seq")
    shards = lax.axis_size("seq")
    member = lax.axis_index("vocab")
    members = lax.axis_size("vocab")
    per_shard, block_len, latent = latent_cache.shape
    rows, heads, _ = query.shape
    value = d_out.shape[2]
    groups, select = block_lists.shape
    qgroup = rows // groups
    part_len = block_len // members
    groups_mine = groups // members
    slots = shards * CAP

    quarter = lax.dynamic_slice_in_dim(latent_cache, member * part_len, part_len, 1)
    table = lax.all_gather(quarter, "seq", axis=0, tiled=True)

    q = lax.all_to_all(
        query.reshape(members, rows // members, heads, latent), "vocab", 0, 0, tiled=True
    )
    d = lax.all_to_all(
        d_out.reshape(members, rows // members, heads, value), "vocab", 0, 0, tiled=True
    )

    flat = block_lists.reshape(-1)
    owner = jnp.where(flat >= 0, flat // per_shard, -1)
    remote = (flat >= 0) & (owner != shard)
    every_block = jnp.arange(shards * per_shard, dtype=jnp.int32)
    matches = flat[:, None] == every_block[None, :]
    present = jnp.any(matches & remote[:, None], axis=0).astype(jnp.int32).reshape(shards, per_shard)
    rank = jnp.cumsum(present, axis=1)
    wanted_rank = jnp.arange(1, CAP + 1, dtype=jnp.int32)[None, :, None]
    slot_hit = present[:, None, :] * (rank[:, None, :] == wanted_rank).astype(jnp.int32)
    requests = (
        jnp.sum(slot_hit * jnp.arange(per_shard, dtype=jnp.int32)[None, None, :], axis=2)
        + jnp.sum(slot_hit, axis=2)
        - 1
    )
    incoming = lax.all_to_all(requests, "seq", split_axis=0, concat_axis=0, tiled=True)
    slot_rank = jnp.sum(matches.astype(jnp.int32) * rank.reshape(-1)[None, :], axis=1)
    table_index = jnp.where(
        owner == shard, flat - shard * per_shard, per_shard + owner * CAP + slot_rank - 1
    )
    table_index = jnp.where(flat >= 0, table_index, 0)
    incoming_index = jnp.where(incoming >= 0, incoming, per_shard).reshape(-1)

    picked = table[jnp.maximum(flat, 0)]
    keys = lax.all_to_all(
        picked.reshape(members, groups_mine * select, part_len, latent), "vocab", 0, 0, tiled=True
    )

    mine = lax.dynamic_slice_in_dim(block_lists, member * groups_mine, groups_mine, 0)
    part_start = jnp.arange(members, dtype=jnp.int32) * part_len
    start = jnp.where(
        mine[:, None, :] >= 0, mine[:, None, :] * block_len + part_start[None, :, None], 1 << 30
    ).reshape(groups_mine, members * select)
    first = shard * (per_shard * block_len) + per_shard * block_len - rows + member * groups_mine * qgroup
    grad_q, grad_keys = attention(start, first.reshape(1), q, d, keys, groups_mine)

    entries = lax.all_to_all(grad_keys, "vocab", 0, 0, tiled=True)
    grad_query = lax.all_to_all(grad_q, "vocab", 0, 0, tiled=True).reshape(rows, heads, latent)
    local, outgoing = sum_by_block(
        table_index, entries.reshape(groups * select, part_len, latent), per_shard, slots
    )
    arrived = lax.all_to_all(
        outgoing.reshape(shards, CAP, part_len, latent), "seq", 0, 0, tiled=True
    ).reshape(slots, part_len, latent)
    grad_cache = receive(incoming_index, arrived, local)
    return grad_query, grad_cache


def solution(mesh):
    in_specs = (
        P("seq", "vocab", None),
        P("seq", None, None),
        P("seq", None),
        P("seq", "vocab", None),
    )
    out_specs = (P("seq", "vocab", None), P("seq", "vocab", None))
    return jax.shard_map(body, mesh=mesh, in_specs=in_specs, out_specs=out_specs, check_vma=False)
```

```python
import functools

import jax
import jax.numpy as jnp
from jax import lax
from jax.experimental import pallas as pl
from jax.experimental.pallas import tpu as pltpu
from jax.sharding import PartitionSpec as P

CAP = 2
SCALE = 0.07216878364870323
LOG2E = 1.4426950408889634
VMEM = 60 * 1024 * 1024


def attention_kernel(members, start_ref, first_ref, row_ref, *refs):
    q_refs, d_refs, k_refs = refs[:members], refs[members : 2 * members], refs[2 * members : 3 * members]
    gq_refs, gk_refs = refs[3 * members : 4 * members], refs[4 * members : 5 * members]
    q_buf, d_buf, k_buf, gq_buf, gk_buf, acc_ref, in_sems, out_sems = refs[5 * members :]
    _, entries, part_len, latent = k_buf.shape
    _, rows, heads, value = d_buf.shape
    part = entries * part_len
    cols = rows * heads
    mine = [pl.ds(row_ref[i], rows) for i in range(members)]
    k_in = [pltpu.make_async_copy(k_refs[i], k_buf.at[i], in_sems.at[i]) for i in range(members)]
    q_in = [
        pltpu.make_async_copy(q_refs[i].at[mine[i]], q_buf.at[i], in_sems.at[members + i])
        for i in range(members)
    ]
    d_in = [
        pltpu.make_async_copy(d_refs[i].at[mine[i]], d_buf.at[i], in_sems.at[2 * members + i])
        for i in range(members)
    ]
    gq_out = [pltpu.make_async_copy(gq_buf.at[i], gq_refs[i], out_sems.at[i]) for i in range(members)]
    gk_out = [
        pltpu.make_async_copy(gk_buf.at[i], gk_refs[i], out_sems.at[members + i])
        for i in range(members)
    ]
    for copy in [q_in[0]] + k_in + [d_in[0]] + q_in[1:] + d_in[1:]:
        copy.start()
    for copy in k_in:
        copy.wait()
    keys = k_buf[...].reshape(members * part, latent)
    nt = (((1,), (1,)), ((), ()))
    shape = (part_len, cols)
    limit = first_ref[0] + lax.broadcasted_iota(jnp.int32, shape, 1) // heads
    limit = limit - lax.broadcasted_iota(jnp.int32, shape, 0)
    for tile in range(members):
        q_in[tile].wait()
        d_in[tile].wait()
        q = q_buf[tile].reshape(cols, latent)
        d = d_buf[tile].reshape(cols, value)
        scores = lax.dot_general(keys, q, nt, preferred_element_type=jnp.float32)
        grad_probs = lax.dot_general(keys[:, :value], d, nt, preferred_element_type=jnp.float32)
        strips = []
        for i in range(members * entries):
            strip = scores[i * part_len : (i + 1) * part_len]
            strips.append(jnp.where(start_ref[i] <= limit, strip, -jnp.inf))
        masked = jnp.concatenate(strips, axis=0)
        top = jnp.max(masked, axis=0, keepdims=True)
        expo = jnp.exp2((masked - top) * (SCALE * LOG2E))
        inverse = 1.0 / jnp.sum(expo, axis=0, keepdims=True)
        delta = jnp.sum(expo * grad_probs, axis=0, keepdims=True) * inverse
        probs_low = (expo * inverse).astype(jnp.bfloat16)
        grad_low = (expo * (inverse * SCALE) * (grad_probs - delta)).astype(jnp.bfloat16)
        gq = lax.dot_general(
            grad_low, keys, (((0,), (0,)), ((), ())), preferred_element_type=jnp.float32
        )
        gq_buf[tile] = gq.astype(jnp.bfloat16).reshape(rows, heads, latent)
        gq_out[tile].start()
        gk = jnp.dot(grad_low, q, preferred_element_type=jnp.float32)
        gv = jnp.dot(probs_low, d, preferred_element_type=jnp.float32)
        if tile == 0:
            acc_ref[...] = gk
        else:
            acc_ref[...] += gk
        acc_ref[:, :value] += gv
    for i in range(members):
        total = acc_ref[i * part : (i + 1) * part]
        gk_buf[i] = total.astype(jnp.bfloat16).reshape(entries, part_len, latent)
        gk_out[i].start()
    for copy in gq_out + gk_out:
        copy.wait()


def attention(start, first, row, q, d, keys):
    members = len(q)
    entries, part_len, latent = keys[0].shape
    _, heads, value = d[0].shape
    rows = entries
    keys_n = members * entries * part_len
    flops = 2 * members * rows * heads * keys_n * (3 * latent + 2 * value)
    smem, hbm = pl.BlockSpec(memory_space=pltpu.SMEM), pl.BlockSpec(memory_space=pltpu.HBM)
    low = jnp.bfloat16
    out = pl.pallas_call(
        functools.partial(attention_kernel, members),
        in_specs=[smem] * 3 + [hbm] * (3 * members),
        out_specs=[hbm] * (2 * members),
        out_shape=[jax.ShapeDtypeStruct((rows, heads, latent), low)] * members
        + [jax.ShapeDtypeStruct(keys[0].shape, low)] * members,
        scratch_shapes=[
            pltpu.VMEM((members, rows, heads, latent), low),
            pltpu.VMEM((members, rows, heads, value), low),
            pltpu.VMEM((members, entries, part_len, latent), low),
            pltpu.VMEM((members, rows, heads, latent), low),
            pltpu.VMEM((members, entries, part_len, latent), low),
            pltpu.VMEM((keys_n, latent), jnp.float32),
            pltpu.SemaphoreType.DMA((3 * members,)),
            pltpu.SemaphoreType.DMA((2 * members,)),
        ],
        compiler_params=pltpu.CompilerParams(vmem_limit_bytes=VMEM),
        cost_estimate=pl.CostEstimate(flops=flops, bytes_accessed=8 << 20, transcendentals=1 << 20),
    )(start, first, row, *q, *d, *keys)
    return out[:members], out[members:]


def sum_by_block_kernel(index_ref, *refs):
    local_ref, slots_ref, table_ref, low_ref, sems = refs[-5:]
    table_ref[...] = jnp.zeros_like(table_ref)
    base = 0
    for in_ref in refs[:-5]:

        def add(i, carry, in_ref=in_ref, base=base):
            table_ref[index_ref[base + i]] += in_ref[i].astype(jnp.float32)
            return carry

        lax.fori_loop(0, in_ref.shape[0], add, 0)
        base += in_ref.shape[0]
    per, slots = local_ref.shape[0], slots_ref.shape[0]
    copies = [pltpu.make_async_copy(table_ref.at[pl.ds(0, per)], local_ref, sems.at[0])]
    copies[0].start()
    chunks = sems.shape[0] - 1
    each = slots // chunks
    part_len, value = table_ref.shape[1], (table_ref.shape[2] // 128) * 128
    for c in range(chunks):

        def pack(i, carry):
            two = [table_ref[per + CAP * i + j].astype(jnp.bfloat16) for j in range(CAP)]
            r = 0
            for x in two:
                for lane in range(0, value, 128):
                    low_ref[i, r : r + part_len] = x[:, lane : lane + 128]
                    r += part_len
            low_ref[i, r : r + part_len] = jnp.concatenate([x[:, value:] for x in two], axis=1)
            return carry

        lax.fori_loop(c * each, (c + 1) * each, pack, 0, unroll=4)
        here = pl.ds(c * each, each)
        copies.append(pltpu.make_async_copy(low_ref.at[here], slots_ref.at[here], sems.at[1 + c]))
        copies[-1].start()
    for copy in copies:
        copy.wait()


def sum_by_block(index, pieces, per_shard, owners):
    _, part_len, latent = pieces[0].shape
    packed = CAP * part_len * latent // 128
    vmem = pl.BlockSpec(memory_space=pltpu.VMEM)
    hbm = pl.BlockSpec(memory_space=pltpu.HBM)
    return pl.pallas_call(
        sum_by_block_kernel,
        in_specs=[pl.BlockSpec(memory_space=pltpu.SMEM)] + [vmem] * len(pieces),
        out_specs=[hbm] * 2,
        out_shape=[
            jax.ShapeDtypeStruct((per_shard, part_len, latent), jnp.float32),
            jax.ShapeDtypeStruct((owners, packed, 128), jnp.bfloat16),
        ],
        scratch_shapes=[
            pltpu.VMEM((per_shard + CAP * owners, part_len, latent), jnp.float32),
            pltpu.VMEM((owners, packed, 128), jnp.bfloat16),
            pltpu.SemaphoreType.DMA((5,)),
        ],
        compiler_params=pltpu.CompilerParams(vmem_limit_bytes=VMEM),
        cost_estimate=pl.CostEstimate(flops=2 << 20, bytes_accessed=6 << 20, transcendentals=0),
    )(index, *pieces)


def receive_kernel(index_ref, in_ref, local_ref, out_ref, table_ref, rest_ref):
    per, part_len, latent = local_ref.shape
    value = (latent // 128) * 128
    rest = latent - value
    last = CAP * part_len * (value // 128)
    table_ref[:per] = local_ref[:, :, :value]
    rest_ref[...] = jnp.zeros_like(rest_ref)

    def add(i, carry):
        for j in range(CAP):
            at = index_ref[CAP * i + j]
            r = j * part_len * (value // 128)
            for lane in range(0, value, 128):
                table_ref[at, :, lane : lane + 128] += in_ref[i, r : r + part_len].astype(jnp.float32)
                r += part_len
            rest_ref[j, at] += in_ref[i, last : last + part_len].astype(jnp.float32)
        return carry

    lax.fori_loop(0, in_ref.shape[0], add, 0, unroll=2)
    out_ref[:, :, :value] = table_ref[:per]
    total = local_ref[:, :, value:]
    for j in range(CAP):
        total += rest_ref[j, :per, :, j * rest : (j + 1) * rest]
    out_ref[:, :, value:] = total


def receive(index, arrived, local):
    per, part_len, latent = local.shape
    return pl.pallas_call(
        receive_kernel,
        in_specs=[
            pl.BlockSpec(memory_space=pltpu.SMEM),
            pl.BlockSpec(memory_space=pltpu.VMEM),
            pl.BlockSpec(memory_space=pltpu.VMEM),
        ],
        out_specs=pl.BlockSpec(memory_space=pltpu.VMEM),
        out_shape=jax.ShapeDtypeStruct(local.shape, jnp.float32),
        scratch_shapes=[
            pltpu.VMEM((per + 1, part_len, latent // 128 * 128), jnp.float32),
            pltpu.VMEM((CAP, per + 1, part_len, 128), jnp.float32),
        ],
        compiler_params=pltpu.CompilerParams(vmem_limit_bytes=12 * 1024 * 1024),
        cost_estimate=pl.CostEstimate(flops=2 << 20, bytes_accessed=4 << 20, transcendentals=0),
    )(index, arrived, local)


def split_kernel(row_ref, in_ref, *refs):
    outs, (buf, sems) = refs[:-2], refs[-2:]
    count, rows = len(outs), outs[0].shape[0]
    ins = [
        pltpu.make_async_copy(in_ref.at[pl.ds(row_ref[k], rows)], buf.at[k], sems.at[k])
        for k in range(count)
    ]
    backs = [pltpu.make_async_copy(buf.at[k], outs[k], sems.at[count + k]) for k in range(count)]
    for copy in ins:
        copy.start()
    for copy, back in zip(ins, backs):
        copy.wait()
        back.start()
    for back in backs:
        back.wait()


def split_rows(row, x, rows):
    count = row.shape[0]
    hbm = pl.BlockSpec(memory_space=pltpu.HBM)
    shape = (rows,) + x.shape[1:]
    return pl.pallas_call(
        split_kernel,
        in_specs=[pl.BlockSpec(memory_space=pltpu.SMEM), hbm],
        out_specs=[hbm] * count,
        out_shape=[jax.ShapeDtypeStruct(shape, x.dtype)] * count,
        scratch_shapes=[
            pltpu.VMEM((count,) + shape, x.dtype),
            pltpu.SemaphoreType.DMA((2 * count,)),
        ],
        compiler_params=pltpu.CompilerParams(vmem_limit_bytes=VMEM),
        cost_estimate=pl.CostEstimate(flops=0, bytes_accessed=4 << 20, transcendentals=0),
    )(row, x)


def join_kernel(row_ref, *refs):
    out_ref = refs[-1]
    for k, ref in enumerate(refs[:-1]):
        out_ref[pl.ds(row_ref[k], ref.shape[0])] = ref[...]


def join_rows(row, pieces):
    rows = sum(p.shape[0] for p in pieces)
    vmem = pl.BlockSpec(memory_space=pltpu.VMEM)
    return pl.pallas_call(
        join_kernel,
        in_specs=[pl.BlockSpec(memory_space=pltpu.SMEM)] + [vmem] * len(pieces),
        out_specs=vmem,
        out_shape=jax.ShapeDtypeStruct((rows,) + pieces[0].shape[1:], pieces[0].dtype),
        compiler_params=pltpu.CompilerParams(vmem_limit_bytes=VMEM),
        cost_estimate=pl.CostEstimate(flops=0, bytes_accessed=5 << 20, transcendentals=0),
    )(row, *pieces)


def pick_kernel(tables, pieces, index_ref, *refs):
    ins, outs = refs[:tables], refs[tables : tables + pieces]
    table_buf, piece_buf, in_sems, out_sems = refs[tables + pieces :]
    each = piece_buf.shape[1]
    copies, base = [], 0
    for t, ref in enumerate(ins):
        dst = table_buf.at[pl.ds(base, ref.shape[0])]
        copies.append(pltpu.make_async_copy(ref, dst, in_sems.at[t]))
        base += ref.shape[0]
    for copy in copies:
        copy.start()
    for copy in copies:
        copy.wait()
    backs = []
    for k in range(pieces):

        def move(i, carry, k=k):
            piece_buf[k, i] = table_buf[index_ref[k * each + i]]
            return carry

        lax.fori_loop(0, each, move, 0, unroll=8)
        backs.append(pltpu.make_async_copy(piece_buf.at[k], outs[k], out_sems.at[k]))
        backs[-1].start()
    for back in backs:
        back.wait()


def pick(index, tables, pieces, each):
    hbm = pl.BlockSpec(memory_space=pltpu.HBM)
    tail, dtype = tables[0].shape[1:], tables[0].dtype
    return pl.pallas_call(
        functools.partial(pick_kernel, len(tables), pieces),
        in_specs=[pl.BlockSpec(memory_space=pltpu.SMEM)] + [hbm] * len(tables),
        out_specs=[hbm] * pieces,
        out_shape=[jax.ShapeDtypeStruct((each,) + tail, dtype)] * pieces,
        scratch_shapes=[
            pltpu.VMEM((sum(t.shape[0] for t in tables),) + tail, dtype),
            pltpu.VMEM((pieces, each) + tail, dtype),
            pltpu.SemaphoreType.DMA((len(tables),)),
            pltpu.SemaphoreType.DMA((pieces,)),
        ],
        compiler_params=pltpu.CompilerParams(vmem_limit_bytes=VMEM),
        cost_estimate=pl.CostEstimate(flops=0, bytes_accessed=4 << 20, transcendentals=0),
    )(index, *tables)


def body(query, latent_cache, block_lists, d_out):
    ax, az, ac = lax.axis_index("x"), lax.axis_index("z"), lax.axis_index("core")
    nx, nz, nc = lax.axis_size("x"), lax.axis_size("z"), lax.axis_size("core")
    shards = nx * nz * nc
    shard = (ax * nz + az) * nc + ac
    member = lax.axis_index("vocab")
    members = lax.axis_size("vocab")
    per_shard, block_len, latent = latent_cache.shape
    rows, heads, _ = query.shape
    groups, select = block_lists.shape
    qgroup = rows // groups
    part_len = block_len // members
    groups_mine = groups // members
    slots = shards * CAP
    barrier = lax.optimization_barrier
    ahead = [lax.rem(member + k, members) for k in range(members)]
    behind = [lax.rem(member - k + members, members) for k in range(members)]

    def ring(x, axis, size, k):
        return lax.ppermute(x, axis, [(i, (i + k) % size) for i in range(size)])

    def shift(x, k):
        return x if k % members == 0 else ring(x, "vocab", members, k)

    flat = block_lists.reshape(-1)
    owner = jnp.where(flat >= 0, flat // per_shard, -1)
    local = owner == shard

    def ranks(entries, blocks, cols):
        matches = entries[..., None] == blocks
        present = jnp.any(matches, axis=-2).astype(jnp.int32)
        rank = jnp.cumsum(present.reshape(present.shape[:-1] + (cols, per_shard)), axis=-1)
        return matches, present.reshape(rank.shape), rank

    every_block = jnp.arange(shards * per_shard, dtype=jnp.int32)
    matches, _, rank = ranks(flat, every_block, shards)
    slot_rank = jnp.sum(matches.astype(jnp.int32) * rank.reshape(-1)[None, :], axis=1) - 1
    own_block = flat - shard * per_shard
    table_index = jnp.where(local, own_block, per_shard + owner * CAP + slot_rank)
    table_index = jnp.where(flat >= 0, table_index, 0).reshape(groups, select)
    owner_x, owner_z, owner_c = owner // (nz * nc), owner // nc % nz, owner % nc
    fetch_index = ((owner_x * nc + owner_c) * nz + owner_z) * CAP + slot_rank
    fetch_index = jnp.where(local, slots + own_block, fetch_index)
    fetch_index = jnp.where(flat >= 0, fetch_index, slots).reshape(groups, select)

    peers = nx * nc
    both = jnp.stack([flat, ring(flat, "core", nc, 1)])
    near = jnp.stack([both] + [ring(both, "x", nx, -k) for k in range(1, nx)])
    turn = lax.rem(jnp.arange(nx, dtype=jnp.int32) - ax + nx, nx)
    swap = lax.rem(jnp.arange(nc, dtype=jnp.int32) + ac, nc)
    near = near[turn][:, swap].reshape(peers, groups * select)
    line_owner = (ax * nz + jnp.arange(nz, dtype=jnp.int32)) * nc + ac
    line_block = (line_owner[:, None] * per_shard + jnp.arange(per_shard, dtype=jnp.int32)).reshape(-1)
    _, present, rank = ranks(near, line_block, nz)
    hit = present[:, :, None, :] * (rank[:, :, None, :] == jnp.arange(1, CAP + 1)[:, None])
    block_of = jnp.arange(per_shard, dtype=jnp.int32)
    asked = jnp.sum(hit * block_of, axis=-1) + jnp.sum(hit, axis=-1) - 1

    quarter = lax.dynamic_slice_in_dim(latent_cache, member * part_len, part_len, 1)
    line = lax.all_to_all(jnp.broadcast_to(quarter, (nz,) + quarter.shape), "z", 0, 0, tiled=True)
    line = line.reshape(nz * per_shard, part_len, latent)

    row_ahead = jnp.stack(ahead) * (rows // members)
    d_sent = split_rows(row_ahead[1:], d_out, rows // members)
    d = [d_out] + [shift(d_sent[k - 1], k) for k in range(1, members)]
    q_sent = split_rows(row_ahead[1:], query, rows // members)

    base = jnp.arange(nz, dtype=jnp.int32) * per_shard
    line_index = (base[None, :, None] + jnp.maximum(asked, 0)).reshape(-1)
    line, d[1:], q_sent = barrier((line, d[1:], q_sent))
    q = [query] + [shift(q_sent[k - 1], k) for k in range(1, members)]
    sent = pick(line_index, [line], 1, peers * nz * CAP)[0]
    table = lax.all_to_all(
        sent.reshape(peers, nz * CAP, part_len, latent), ("x", "core"), 0, 0, tiled=True
    ).reshape(slots, part_len, latent)

    first_row = (shard + 1) * (per_shard * block_len) - rows
    part_start = jnp.stack(behind) * part_len
    list_ids = [jnp.stack(ahead) * groups_mine + g for g in range(groups_mine)]
    table, q[1:] = barrier((table, q[1:]))
    keys = []
    for g in range(groups_mine):
        index = fetch_index[list_ids[g]].reshape(-1)
        picked = pick(index, [table, quarter], members, select)
        keys.append([shift(picked[k], k) for k in range(members)])
    grad_q, entries = [], []
    for g in range(groups_mine):
        mine = lax.dynamic_index_in_dim(block_lists, member * groups_mine + g, 0, keepdims=False)
        start = jnp.where(
            mine[None, :] >= 0, mine[None, :] * block_len + part_start[:, None], 1 << 30
        ).reshape(-1)
        first = first_row + (member * groups_mine + g) * qgroup
        row = [member * (rows // members)] + [jnp.int32(0)] * (members - 1)
        row = jnp.stack(row) + g * qgroup
        gq, gk = attention(start, first.reshape(1), row, q, d, keys[g])
        grad_q.append(gq)
        if g < groups_mine - 1:
            gk = [shift(gk[k], -k) for k in range(members)]
        entries += gk
    asked, entries[-members:] = barrier((asked, entries[-members:]))
    incoming = lax.all_to_all(asked.transpose(1, 0, 2), "z", 0, 0, tiled=True)
    incoming = incoming.reshape(nz, nx, nc, CAP).transpose(1, 0, 2, 3).reshape(-1)
    incoming_index = jnp.where(incoming >= 0, incoming, per_shard)
    entries[-members:] = [shift(entries[k - members], -k) for k in range(members)]
    entry_index = jnp.concatenate([table_index[ids].reshape(-1) for ids in list_ids])

    entry_index, incoming_index = barrier((entry_index, incoming_index))
    local_grad, outgoing = sum_by_block(entry_index, entries, per_shard, shards)
    arrived = lax.all_to_all(outgoing, ("x", "z", "core"), 0, 0, tiled=True)
    grad_cache = receive(incoming_index, arrived, local_grad)

    grad_q, _ = barrier((grad_q, outgoing))
    pieces = [shift(grad_q[g][k], -k) for g in range(groups_mine) for k in range(members)]
    place = jnp.concatenate([row_ahead + g * qgroup for g in range(groups_mine)])
    grad_query = join_rows(place, pieces)
    return grad_query, grad_cache


def solution(mesh):
    names = ("x", "z", "core", "vocab")
    mesh = jax.sharding.Mesh(mesh.devices.reshape(4, 8, 2, 4), names)
    seq = names[:3]
    in_specs = (P(seq, "vocab", None), P(seq, None, None), P(seq, None), P(seq, "vocab", None))
    out_specs = (P(seq, "vocab", None), P(seq, "vocab", None))
    return jax.shard_map(body, mesh=mesh, in_specs=in_specs, out_specs=out_specs, check_vma=False)
```

```python
import functools

import jax
import jax.numpy as jnp
from jax import lax
from jax.experimental import pallas as pl
from jax.experimental.pallas import tpu as pltpu
from jax.sharding import PartitionSpec as P

CAP = 2
SCALE = 0.07216878364870323
LOG2E = 1.4426950408889634
VMEM = 60 * 1024 * 1024


def swap_halves(x):
    half = x.shape[1] // 2
    return jnp.concatenate([x[:, half:], x[:, :half]], axis=1)


def pack_pair(two, dst_ref, at):
    tokens, latent = two[0].shape
    value = latent // 128 * 128
    r = 0
    for x in two:
        for lane in range(0, value, 128):
            dst_ref[at + (slice(r, r + tokens),)] = x[:, lane : lane + 128]
            r += tokens
    dst_ref[at + (slice(r, r + tokens),)] = jnp.concatenate([x[:, value:] for x in two], axis=1)


def attention_kernel(members, start_ref, first_ref, row_ref, *refs):
    q_refs, d_refs, k_refs = refs[:members], refs[members : 2 * members], refs[2 * members : 3 * members]
    gq_refs, gk_refs = refs[3 * members : 4 * members], refs[4 * members : 5 * members]
    q_buf, d_buf, k_buf, gq_buf, gk_buf, q_packed, keys_ref, p_ref, g_ref, in_sems, out_sems = refs[5 * members :]
    _, rows, heads, latent = q_buf.shape
    value = d_buf.shape[3]
    pairs, part_len = k_buf.shape[1], k_buf.shape[2] * 128 // (CAP * latent)
    entries = CAP * pairs
    part = entries * part_len
    cols = rows * heads
    mine = [pl.ds(row_ref[i], rows) for i in range(members)]
    k_in = [pltpu.make_async_copy(k_refs[i], k_buf.at[i], in_sems.at[i]) for i in range(members)]
    q_in = [pltpu.make_async_copy(q_refs[0].at[mine[0]], q_buf.at[0], in_sems.at[members])]
    for i in range(1, members):
        src = q_refs[i].at[pl.ds(row_ref[i] // CAP, rows // CAP)]
        q_in.append(pltpu.make_async_copy(src, q_packed.at[i - 1], in_sems.at[members + i]))
    d_in = [
        pltpu.make_async_copy(d_refs[i].at[mine[i]], d_buf.at[i], in_sems.at[2 * members + i])
        for i in range(members)
    ]
    gq_out = [pltpu.make_async_copy(gq_buf.at[i], gq_refs[i], out_sems.at[i]) for i in range(members)]
    gk_out = [
        pltpu.make_async_copy(gk_buf.at[i], gk_refs[i], out_sems.at[members + i])
        for i in range(members)
    ]
    for copy in [q_in[0]] + k_in + [d_in[0]] + q_in[1:] + d_in[1:]:
        copy.start()
    whole = part_len * (value // 128)
    for i in range(members):
        k_in[i].wait()
        for pair in range(pairs):
            rest = k_buf[i, pair, CAP * whole : CAP * whole + part_len]
            for j in range(CAP):
                r = i * part + (CAP * pair + j) * part_len
                for lane in range(0, value, 128):
                    c = j * whole + lane // 128 * part_len
                    keys_ref[r : r + part_len, lane : lane + 128] = k_buf[i, pair, c : c + part_len]
                width = latent - value
                keys_ref[r : r + part_len, value:] = rest[:, j * width : (j + 1) * width]
    keys = keys_ref[...]
    nt = (((1,), (1,)), ((), ()))
    shape = (part_len, cols)
    limit = first_ref[0] + lax.broadcasted_iota(jnp.int32, shape, 1) // heads
    limit = limit - lax.broadcasted_iota(jnp.int32, shape, 0)
    def load(tile):
        q_in[tile].wait()
        if tile > 0:
            whole_q = heads * (value // 128)
            for pair in range(rows // CAP):
                rest = q_packed[tile - 1, pair, CAP * whole_q : CAP * whole_q + heads]
                for j in range(CAP):
                    r = CAP * pair + j
                    for lane in range(0, value, 128):
                        c = j * whole_q + lane // 128 * heads
                        q_buf[tile, r, :, lane : lane + 128] = q_packed[tile - 1, pair, c : c + heads]
                    width = latent - value
                    q_buf[tile, r, :, value:] = rest[:, j * width : (j + 1) * width]
        d_in[tile].wait()
        q = q_buf[tile].reshape(cols, latent)
        d = d_buf[tile].reshape(cols, value)
        scores = lax.dot_general(keys, q, nt, preferred_element_type=jnp.float32)
        grad_probs = lax.dot_general(keys[:, :value], d, nt, preferred_element_type=jnp.float32)
        return q, d, scores, grad_probs

    ahead = load(0)
    for tile in range(members):
        q, d, scores, grad_probs = ahead
        strips = []
        for i in range(members * entries):
            strip = scores[i * part_len : (i + 1) * part_len]
            strips.append(jnp.where(start_ref[i] <= limit, strip, -jnp.inf))
        masked = jnp.concatenate(strips, axis=0)
        top = jnp.max(masked, axis=0, keepdims=True)
        expo = jnp.exp2((masked - top) * (SCALE * LOG2E))
        inverse = 1.0 / jnp.sum(expo, axis=0, keepdims=True)
        delta = jnp.sum(expo * grad_probs, axis=0, keepdims=True) * inverse
        probs_low = (expo * inverse).astype(jnp.bfloat16)
        grad_low = (expo * (inverse * SCALE) * (grad_probs - delta)).astype(jnp.bfloat16)
        if tile + 1 < members:
            ahead = load(tile + 1)
        gq = lax.dot_general(
            grad_low, keys, (((0,), (0,)), ((), ())), preferred_element_type=jnp.float32
        )
        gq_buf[tile] = gq.astype(jnp.bfloat16).reshape(rows, heads, latent)
        gq_out[tile].start()
        p_ref[:, tile * cols : (tile + 1) * cols] = probs_low
        g_ref[:, tile * cols : (tile + 1) * cols] = grad_low
    q_all = q_buf[...].reshape(members * cols, latent)
    d_all = d_buf[...].reshape(members * cols, value)
    for i in range(members):
        here = slice(i * part, (i + 1) * part)
        gk = jnp.dot(g_ref[here], q_all, preferred_element_type=jnp.float32)
        gv = jnp.dot(p_ref[here], d_all, preferred_element_type=jnp.float32)
        total = jnp.concatenate([gk[:, :value] + gv, gk[:, value:]], axis=1)
        total = total.astype(jnp.bfloat16)
        for pair in range(pairs):
            r = CAP * pair * part_len
            two = [total[r + j * part_len : r + (j + 1) * part_len] for j in range(CAP)]
            pack_pair(two, gk_buf, (i, pair))
        gk_out[i].start()
    for copy in gq_out + gk_out:
        copy.wait()


def attention(start, first, row, q, d, keys):
    members = len(q)
    pairs, packed, _ = keys[0].shape
    _, heads, value = d[0].shape
    latent = q[0].shape[2]
    rows = CAP * pairs
    keys_n = members * pairs * packed * 128 // latent
    flops = 2 * members * rows * heads * keys_n * (3 * latent + 2 * value)
    smem, hbm = pl.BlockSpec(memory_space=pltpu.SMEM), pl.BlockSpec(memory_space=pltpu.HBM)
    low = jnp.bfloat16
    out = pl.pallas_call(
        functools.partial(attention_kernel, members),
        in_specs=[smem] * 3 + [hbm] * (3 * members),
        out_specs=[hbm] * (2 * members),
        out_shape=[jax.ShapeDtypeStruct((rows, heads, latent), low)] * members
        + [jax.ShapeDtypeStruct(keys[0].shape, low)] * members,
        scratch_shapes=[
            pltpu.VMEM((members, rows, heads, latent), low),
            pltpu.VMEM((members, rows, heads, value), low),
            pltpu.VMEM((members, pairs, packed, 128), low),
            pltpu.VMEM((members, rows, heads, latent), low),
            pltpu.VMEM((members, pairs, packed, 128), low),
            pltpu.VMEM((members - 1, rows // CAP) + q[1].shape[1:], low),
            pltpu.VMEM((keys_n, latent), low),
            pltpu.VMEM((keys_n, members * rows * heads), low),
            pltpu.VMEM((keys_n, members * rows * heads), low),
            pltpu.SemaphoreType.DMA((3 * members,)),
            pltpu.SemaphoreType.DMA((2 * members,)),
        ],
        compiler_params=pltpu.CompilerParams(vmem_limit_bytes=VMEM),
        cost_estimate=pl.CostEstimate(flops=flops, bytes_accessed=8 << 20, transcendentals=1 << 20),
    )(start, first, row, *q, *d, *keys)
    return out[:members], out[members:]


def sum_by_block_kernel(count, index_ref, *refs):
    ins, rest_refs = refs[:count], refs[count:]
    local_ref, slots_ref, table_ref, rest_ref, local_buf, low_ref, sems = rest_refs
    pairs = ins[0].shape[0]
    per, part_len, latent = local_buf.shape
    value = table_ref.shape[2]
    width = latent - value
    whole = part_len * (value // 128)
    table_ref[...] = jnp.zeros_like(table_ref)
    rest_ref[...] = jnp.zeros_like(rest_ref)
    for k in range(count):

        def add(i, carry, k=k):
            rest = ins[k][i, CAP * whole : CAP * whole + part_len].astype(jnp.float32)
            for j in range(CAP):
                at = index_ref[CAP * (k * pairs + i) + j]
                for lane in range(0, value, 128):
                    c = j * whole + lane // 128 * part_len
                    x = ins[k][i, c : c + part_len].astype(jnp.float32)
                    table_ref[at, :, lane : lane + 128] += x
                rest_ref[j, at] += rest
            return carry

        lax.fori_loop(0, pairs, add, 0, unroll=2)
    local_buf[:, :, :value] = table_ref[:per]
    total = rest_ref[0, :per, :, :width]
    for j in range(1, CAP):
        total += rest_ref[j, :per, :, j * width : (j + 1) * width]
    local_buf[:, :, value:] = total
    copies = [pltpu.make_async_copy(local_buf, local_ref, sems.at[0])]
    copies[0].start()
    chunks = sems.shape[0] - 1
    each = slots_ref.shape[0] // chunks
    low_lanes = lax.broadcasted_iota(jnp.int32, (part_len, 128), 1) < width
    for c in range(chunks):

        def pack(i, carry):
            r = 0
            for j in range(CAP):
                for lane in range(0, value, 128):
                    x = table_ref[per + CAP * i + j, :, lane : lane + 128]
                    low_ref[i, r : r + part_len] = x.astype(jnp.bfloat16)
                    r += part_len
            a, b = per + CAP * i, per + CAP * i + 1
            first = rest_ref[0, a] + swap_halves(rest_ref[1, a])
            second = swap_halves(rest_ref[0, b]) + rest_ref[1, b]
            low_ref[i, r : r + part_len] = jnp.where(low_lanes, first, second).astype(jnp.bfloat16)
            return carry

        lax.fori_loop(c * each, (c + 1) * each, pack, 0, unroll=4)
        here = pl.ds(c * each, each)
        copies.append(pltpu.make_async_copy(low_ref.at[here], slots_ref.at[here], sems.at[1 + c]))
        copies[-1].start()
    for copy in copies:
        copy.wait()


def sum_by_block(index, pieces, per_shard, owners, latent):
    packed = pieces[0].shape[1]
    part_len = packed * 128 // (CAP * latent)
    value = latent // 128 * 128
    rows = per_shard + CAP * owners
    vmem = pl.BlockSpec(memory_space=pltpu.VMEM)
    hbm = pl.BlockSpec(memory_space=pltpu.HBM)
    return pl.pallas_call(
        functools.partial(sum_by_block_kernel, len(pieces)),
        in_specs=[pl.BlockSpec(memory_space=pltpu.SMEM)] + [vmem] * len(pieces),
        out_specs=[hbm] * 2,
        out_shape=[
            jax.ShapeDtypeStruct((per_shard, part_len, latent), jnp.float32),
            jax.ShapeDtypeStruct((owners, packed, 128), jnp.bfloat16),
        ],
        scratch_shapes=[
            pltpu.VMEM((rows, part_len, value), jnp.float32),
            pltpu.VMEM((CAP, rows, part_len, 128), jnp.float32),
            pltpu.VMEM((per_shard, part_len, latent), jnp.float32),
            pltpu.VMEM((owners, packed, 128), jnp.bfloat16),
            pltpu.SemaphoreType.DMA((5,)),
        ],
        compiler_params=pltpu.CompilerParams(vmem_limit_bytes=VMEM),
        cost_estimate=pl.CostEstimate(flops=2 << 20, bytes_accessed=6 << 20, transcendentals=0),
    )(index, *pieces)


def receive_kernel(index_ref, in_ref, local_ref, out_ref, table_ref, rest_ref):
    per, part_len, latent = local_ref.shape
    value = (latent // 128) * 128
    rest = latent - value
    last = CAP * part_len * (value // 128)
    table_ref[:per] = local_ref[:, :, :value]
    rest_ref[...] = jnp.zeros_like(rest_ref)

    def add(i, carry):
        for j in range(CAP):
            at = index_ref[CAP * i + j]
            r = j * part_len * (value // 128)
            for lane in range(0, value, 128):
                table_ref[at, :, lane : lane + 128] += in_ref[i, r : r + part_len].astype(jnp.float32)
                r += part_len
            rest_ref[j, at] += in_ref[i, last : last + part_len].astype(jnp.float32)
        return carry

    lax.fori_loop(0, in_ref.shape[0], add, 0, unroll=2)
    out_ref[:, :, :value] = table_ref[:per]
    total = local_ref[:, :, value:]
    for j in range(CAP):
        total += rest_ref[j, :per, :, j * rest : (j + 1) * rest]
    out_ref[:, :, value:] = total


def receive(index, arrived, local):
    per, part_len, latent = local.shape
    return pl.pallas_call(
        receive_kernel,
        in_specs=[
            pl.BlockSpec(memory_space=pltpu.SMEM),
            pl.BlockSpec(memory_space=pltpu.VMEM),
            pl.BlockSpec(memory_space=pltpu.VMEM),
        ],
        out_specs=pl.BlockSpec(memory_space=pltpu.VMEM),
        out_shape=jax.ShapeDtypeStruct(local.shape, jnp.float32),
        scratch_shapes=[
            pltpu.VMEM((per + 1, part_len, latent // 128 * 128), jnp.float32),
            pltpu.VMEM((CAP, per + 1, part_len, 128), jnp.float32),
        ],
        compiler_params=pltpu.CompilerParams(vmem_limit_bytes=12 * 1024 * 1024),
        cost_estimate=pl.CostEstimate(flops=2 << 20, bytes_accessed=4 << 20, transcendentals=0),
    )(index, arrived, local)


def split_kernel(row_ref, in_ref, *refs):
    outs, (buf, sems) = refs[:-2], refs[-2:]
    count, rows = len(outs), outs[0].shape[0]
    ins = [
        pltpu.make_async_copy(in_ref.at[pl.ds(row_ref[k], rows)], buf.at[k], sems.at[k])
        for k in range(count)
    ]
    backs = [pltpu.make_async_copy(buf.at[k], outs[k], sems.at[count + k]) for k in range(count)]
    for copy in ins:
        copy.start()
    for copy, back in zip(ins, backs):
        copy.wait()
        back.start()
    for back in backs:
        back.wait()


def split_rows(row, x, rows):
    count = row.shape[0]
    hbm = pl.BlockSpec(memory_space=pltpu.HBM)
    shape = (rows,) + x.shape[1:]
    return pl.pallas_call(
        split_kernel,
        in_specs=[pl.BlockSpec(memory_space=pltpu.SMEM), hbm],
        out_specs=[hbm] * count,
        out_shape=[jax.ShapeDtypeStruct(shape, x.dtype)] * count,
        scratch_shapes=[
            pltpu.VMEM((count,) + shape, x.dtype),
            pltpu.SemaphoreType.DMA((2 * count,)),
        ],
        compiler_params=pltpu.CompilerParams(vmem_limit_bytes=VMEM),
        cost_estimate=pl.CostEstimate(flops=0, bytes_accessed=4 << 20, transcendentals=0),
    )(row, x)


def split_pack_kernel(row_ref, in_ref, *refs):
    outs, (buf, out_buf, sems) = refs[:-3], refs[-3:]
    count, rows = buf.shape[0], buf.shape[1]
    ins = [
        pltpu.make_async_copy(in_ref.at[pl.ds(row_ref[k], rows)], buf.at[k], sems.at[k])
        for k in range(count)
    ]
    backs = [pltpu.make_async_copy(out_buf.at[k], outs[k], sems.at[count + k]) for k in range(count)]
    for copy in ins:
        copy.start()
    for k in range(count):
        ins[k].wait()

        def move(i, carry, k=k):
            pack_pair([buf[k, CAP * i + j] for j in range(CAP)], out_buf, (k, i))
            return carry

        lax.fori_loop(0, rows // CAP, move, 0, unroll=4)
        backs[k].start()
    for back in backs:
        back.wait()


def split_pack_rows(row, x, rows):
    count = row.shape[0]
    hbm = pl.BlockSpec(memory_space=pltpu.HBM)
    shape = (rows // CAP, CAP * x.shape[1] * x.shape[2] // 128, 128)
    return pl.pallas_call(
        split_pack_kernel,
        in_specs=[pl.BlockSpec(memory_space=pltpu.SMEM), hbm],
        out_specs=[hbm] * count,
        out_shape=[jax.ShapeDtypeStruct(shape, x.dtype)] * count,
        scratch_shapes=[
            pltpu.VMEM((count, rows) + x.shape[1:], x.dtype),
            pltpu.VMEM((count,) + shape, x.dtype),
            pltpu.SemaphoreType.DMA((2 * count,)),
        ],
        compiler_params=pltpu.CompilerParams(vmem_limit_bytes=VMEM),
        cost_estimate=pl.CostEstimate(flops=0, bytes_accessed=4 << 20, transcendentals=0),
    )(row, x)


def join_kernel(row_ref, *refs):
    out_ref = refs[-1]
    for k, ref in enumerate(refs[:-1]):
        out_ref[pl.ds(row_ref[k], ref.shape[0])] = ref[...]


def join_rows(row, pieces):
    rows = sum(p.shape[0] for p in pieces)
    vmem = pl.BlockSpec(memory_space=pltpu.VMEM)
    return pl.pallas_call(
        join_kernel,
        in_specs=[pl.BlockSpec(memory_space=pltpu.SMEM)] + [vmem] * len(pieces),
        out_specs=vmem,
        out_shape=jax.ShapeDtypeStruct((rows,) + pieces[0].shape[1:], pieces[0].dtype),
        compiler_params=pltpu.CompilerParams(vmem_limit_bytes=VMEM),
        cost_estimate=pl.CostEstimate(flops=0, bytes_accessed=5 << 20, transcendentals=0),
    )(row, *pieces)


def ask_kernel(index_ref, line_ref, out_ref, line_buf, out_buf, sems):
    load = pltpu.make_async_copy(line_ref, line_buf, sems.at[0])
    load.start()
    load.wait()

    def move(i, carry):
        pack_pair([line_buf[index_ref[CAP * i + j]] for j in range(CAP)], out_buf, (i,))
        return carry

    chunks = sems.shape[0] - 1
    each = out_ref.shape[0] // chunks
    backs = []
    for c in range(chunks):
        lax.fori_loop(c * each, (c + 1) * each, move, 0, unroll=4)
        here = pl.ds(c * each, each)
        backs.append(pltpu.make_async_copy(out_buf.at[here], out_ref.at[here], sems.at[1 + c]))
        backs[-1].start()
    for back in backs:
        back.wait()


def ask(index, line):
    _, part_len, latent = line.shape
    hbm = pl.BlockSpec(memory_space=pltpu.HBM)
    shape = (index.shape[0] // CAP, CAP * part_len * latent // 128, 128)
    return pl.pallas_call(
        ask_kernel,
        in_specs=[pl.BlockSpec(memory_space=pltpu.SMEM), hbm],
        out_specs=hbm,
        out_shape=jax.ShapeDtypeStruct(shape, line.dtype),
        scratch_shapes=[
            pltpu.VMEM(line.shape, line.dtype),
            pltpu.VMEM(shape, line.dtype),
            pltpu.SemaphoreType.DMA((5,)),
        ],
        compiler_params=pltpu.CompilerParams(vmem_limit_bytes=VMEM),
        cost_estimate=pl.CostEstimate(flops=0, bytes_accessed=4 << 20, transcendentals=0),
    )(index, line)


def pick_kernel(pieces, index_ref, table_ref, own_ref, *refs):
    outs, (table_buf, own_buf, out_buf, in_sems, out_sems) = refs[:pieces], refs[pieces:]
    size, packed = table_ref.shape[0], table_ref.shape[1]
    own, part_len, latent = own_buf.shape
    pairs = out_buf.shape[1]
    whole = part_len * (latent // 128)
    loads = [
        pltpu.make_async_copy(own_ref, own_buf, in_sems.at[0]),
        pltpu.make_async_copy(table_ref, table_buf.at[pl.ds(0, size)], in_sems.at[1]),
    ]
    for load in loads:
        load.start()
    loads[0].wait()
    for i in range(own // CAP):
        pack_pair([own_buf[CAP * i + j] for j in range(CAP)], table_buf, (size + i,))
    loads[1].wait()
    low_lanes = lax.broadcasted_iota(jnp.int32, (part_len, 128), 1) < latent % 128
    backs = []
    for k in range(pieces):

        def move(i, carry, k=k):
            rests = []
            for j in range(CAP):
                e = index_ref[CAP * (k * pairs + i) + j]
                at, side = e // CAP, e % CAP
                src = pl.ds(pl.multiple_of(side * whole, whole), whole)
                out_buf[k, i, j * whole : (j + 1) * whole] = table_buf[at, src]
                rest = table_buf[at, CAP * whole : packed]
                rests.append(jnp.where(side == j, rest, swap_halves(rest)))
            out_buf[k, i, CAP * whole : packed] = jnp.where(low_lanes, rests[0], rests[1])
            return carry

        lax.fori_loop(0, pairs, move, 0, unroll=4)
        backs.append(pltpu.make_async_copy(out_buf.at[k], outs[k], out_sems.at[k]))
        backs[-1].start()
    for back in backs:
        back.wait()


def pick(index, table, own, pieces):
    hbm = pl.BlockSpec(memory_space=pltpu.HBM)
    size, packed, _ = table.shape
    pairs = index.shape[0] // (CAP * pieces)
    return pl.pallas_call(
        functools.partial(pick_kernel, pieces),
        in_specs=[pl.BlockSpec(memory_space=pltpu.SMEM), hbm, hbm],
        out_specs=[hbm] * pieces,
        out_shape=[jax.ShapeDtypeStruct((pairs, packed, 128), table.dtype)] * pieces,
        scratch_shapes=[
            pltpu.VMEM((size + own.shape[0] // CAP, packed, 128), table.dtype),
            pltpu.VMEM(own.shape, own.dtype),
            pltpu.VMEM((pieces, pairs, packed, 128), table.dtype),
            pltpu.SemaphoreType.DMA((2,)),
            pltpu.SemaphoreType.DMA((pieces,)),
        ],
        compiler_params=pltpu.CompilerParams(vmem_limit_bytes=VMEM),
        cost_estimate=pl.CostEstimate(flops=0, bytes_accessed=4 << 20, transcendentals=0),
    )(index, table, own)


def body(query, latent_cache, block_lists, d_out):
    ax, az, ac = lax.axis_index("x"), lax.axis_index("z"), lax.axis_index("core")
    nx, nz, nc = lax.axis_size("x"), lax.axis_size("z"), lax.axis_size("core")
    shards = nx * nz * nc
    shard = (ax * nz + az) * nc + ac
    member = lax.axis_index("vocab")
    members = lax.axis_size("vocab")
    per_shard, block_len, latent = latent_cache.shape
    rows, heads, _ = query.shape
    groups, select = block_lists.shape
    qgroup = rows // groups
    part_len = block_len // members
    groups_mine = groups // members
    slots = shards * CAP
    barrier = lax.optimization_barrier
    ahead = [lax.rem(member + k, members) for k in range(members)]
    behind = [lax.rem(member - k + members, members) for k in range(members)]

    def ring(x, axis, size, k):
        return lax.ppermute(x, axis, [(i, (i + k) % size) for i in range(size)])

    def shift(x, k):
        return x if k % members == 0 else ring(x, "vocab", members, k)

    flat = block_lists.reshape(-1)
    owner = jnp.where(flat >= 0, flat // per_shard, -1)
    local = owner == shard

    def ranks(entries, blocks, cols):
        matches = entries[..., None] == blocks
        present = jnp.any(matches, axis=-2).astype(jnp.int32)
        rank = jnp.cumsum(present.reshape(present.shape[:-1] + (cols, per_shard)), axis=-1)
        return matches, present.reshape(rank.shape), rank

    every_block = jnp.arange(shards * per_shard, dtype=jnp.int32)
    matches, _, rank = ranks(flat, every_block, shards)
    slot_rank = jnp.sum(matches.astype(jnp.int32) * rank.reshape(-1)[None, :], axis=1) - 1
    own_block = flat - shard * per_shard
    table_index = jnp.where(local, own_block, per_shard + owner * CAP + slot_rank)
    table_index = jnp.where(flat >= 0, table_index, 0).reshape(groups, select)
    owner_x, owner_z, owner_c = owner // (nz * nc), owner // nc % nz, owner % nc
    fetch_index = ((owner_x * nc + owner_c) * nz + owner_z) * CAP + slot_rank
    fetch_index = jnp.where(local, slots + own_block, fetch_index)
    fetch_index = jnp.where(flat >= 0, fetch_index, slots).reshape(groups, select)

    peers = nx * nc
    both = jnp.stack([flat, ring(flat, "core", nc, 1)])
    near = jnp.stack([both] + [ring(both, "x", nx, -k) for k in range(1, nx)])
    turn = lax.rem(jnp.arange(nx, dtype=jnp.int32) - ax + nx, nx)
    swap = lax.rem(jnp.arange(nc, dtype=jnp.int32) + ac, nc)
    near = near[turn][:, swap].reshape(peers, groups * select)
    line_owner = (ax * nz + jnp.arange(nz, dtype=jnp.int32)) * nc + ac
    line_block = (line_owner[:, None] * per_shard + jnp.arange(per_shard, dtype=jnp.int32)).reshape(-1)
    _, present, rank = ranks(near, line_block, nz)
    hit = present[:, :, None, :] * (rank[:, :, None, :] == jnp.arange(1, CAP + 1)[:, None])
    block_of = jnp.arange(per_shard, dtype=jnp.int32)
    asked = jnp.sum(hit * block_of, axis=-1) + jnp.sum(hit, axis=-1) - 1

    quarter = lax.dynamic_slice_in_dim(latent_cache, member * part_len, part_len, 1)
    line = lax.all_to_all(jnp.broadcast_to(quarter, (nz,) + quarter.shape), "z", 0, 0, tiled=True)
    line = line.reshape(nz * per_shard, part_len, latent)

    row_ahead = jnp.stack(ahead) * (rows // members)
    d_sent = split_rows(row_ahead[1:], d_out, rows // members)
    d = [d_out] + [shift(d_sent[k - 1], k) for k in range(1, members)]
    q_sent = split_pack_rows(row_ahead[1:], query, rows // members)

    base = jnp.arange(nz, dtype=jnp.int32) * per_shard
    line_index = (base[None, :, None] + jnp.maximum(asked, 0)).reshape(-1)
    line, d[1:], q_sent = barrier((line, d[1:], q_sent))
    q = [query] + [shift(q_sent[k - 1], k) for k in range(1, members)]
    sent = ask(line_index, line)
    table = lax.all_to_all(
        sent.reshape((peers, nz) + sent.shape[1:]), ("x", "core"), 0, 0, tiled=True
    ).reshape(sent.shape)

    first_row = (shard + 1) * (per_shard * block_len) - rows
    part_start = jnp.stack(behind) * part_len
    list_ids = [jnp.stack(ahead) * groups_mine + g for g in range(groups_mine)]
    table, q[1:] = barrier((table, q[1:]))
    keys = []
    for g in range(groups_mine):
        index = fetch_index[list_ids[g]].reshape(-1)
        picked = pick(index, table, quarter, members)
        keys.append([shift(picked[k], k) for k in range(members)])
    grad_q, entries = [], []
    for g in range(groups_mine):
        mine = lax.dynamic_index_in_dim(block_lists, member * groups_mine + g, 0, keepdims=False)
        start = jnp.where(
            mine[None, :] >= 0, mine[None, :] * block_len + part_start[:, None], 1 << 30
        ).reshape(-1)
        first = first_row + (member * groups_mine + g) * qgroup
        row = [member * (rows // members)] + [jnp.int32(0)] * (members - 1)
        row = jnp.stack(row) + g * qgroup
        gq, gk = attention(start, first.reshape(1), row, q, d, keys[g])
        grad_q.append(gq)
        if g < groups_mine - 1:
            gk = [shift(gk[k], -k) for k in range(members)]
        entries += gk
    asked, entries[-members:] = barrier((asked, entries[-members:]))
    incoming = lax.all_to_all(asked.transpose(1, 0, 2), "z", 0, 0, tiled=True)
    incoming = incoming.reshape(nz, nx, nc, CAP).transpose(1, 0, 2, 3).reshape(-1)
    incoming_index = jnp.where(incoming >= 0, incoming, per_shard)
    entries[-members:] = [shift(entries[k - members], -k) for k in range(members)]
    entry_index = jnp.concatenate([table_index[ids].reshape(-1) for ids in list_ids])

    entry_index, incoming_index = barrier((entry_index, incoming_index))
    local_grad, outgoing = sum_by_block(entry_index, entries, per_shard, shards, latent)
    arrived = lax.all_to_all(outgoing, ("x", "z", "core"), 0, 0, tiled=True)
    grad_cache = receive(incoming_index, arrived, local_grad)

    grad_q, _ = barrier((grad_q, outgoing))
    pieces = [shift(grad_q[g][k], -k) for g in range(groups_mine) for k in range(members)]
    place = jnp.concatenate([row_ahead + g * qgroup for g in range(groups_mine)])
    grad_query = join_rows(place, pieces)
    return grad_query, grad_cache


def solution(mesh):
    names = ("x", "z", "core", "vocab")
    mesh = jax.sharding.Mesh(mesh.devices.reshape(4, 8, 2, 4), names)
    seq = names[:3]
    in_specs = (P(seq, "vocab", None), P(seq, None, None), P(seq, None), P(seq, "vocab", None))
    out_specs = (P(seq, "vocab", None), P(seq, "vocab", None))
    return jax.shard_map(body, mesh=mesh, in_specs=in_specs, out_specs=out_specs, check_vma=False)
```

```python
import functools

import jax
import jax.numpy as jnp
from jax import lax
from jax.experimental import pallas as pl
from jax.experimental.pallas import tpu as pltpu
from jax.sharding import PartitionSpec as P

CAP = 2
SCALE = 0.07216878364870323
LOG2E = 1.4426950408889634
VMEM = 60 * 1024 * 1024


def swap_halves(x):
    half = x.shape[1] // 2
    return jnp.concatenate([x[:, half:], x[:, :half]], axis=1)


def pack_pair(two, dst_ref, at):
    tokens, latent = two[0].shape
    value = latent // 128 * 128
    r = 0
    for x in two:
        for lane in range(0, value, 128):
            dst_ref[at + (slice(r, r + tokens),)] = x[:, lane : lane + 128]
            r += tokens
    dst_ref[at + (slice(r, r + tokens),)] = jnp.concatenate([x[:, value:] for x in two], axis=1)


def attention_kernel(members, start_ref, first_ref, row_ref, *refs):
    q_refs, d_refs, k_refs = refs[:members], refs[members : 2 * members], refs[2 * members : 3 * members]
    gq_refs, gk_refs = refs[3 * members : 4 * members], refs[4 * members : 5 * members]
    q_buf, d_buf, k_buf, gq_buf, gk_buf, q_packed, keys_ref, p_ref, g_ref, in_sems, out_sems = refs[5 * members :]
    _, rows, heads, latent = q_buf.shape
    value = d_buf.shape[3]
    pairs, part_len = k_buf.shape[1], k_buf.shape[2] * 128 // (CAP * latent)
    entries = CAP * pairs
    part = entries * part_len
    cols = rows * heads
    mine = [pl.ds(row_ref[i], rows) for i in range(members)]
    k_in = [pltpu.make_async_copy(k_refs[i], k_buf.at[i], in_sems.at[i]) for i in range(members)]
    q_in = [pltpu.make_async_copy(q_refs[0].at[mine[0]], q_buf.at[0], in_sems.at[members])]
    for i in range(1, members):
        src = q_refs[i].at[pl.ds(row_ref[i] // CAP, rows // CAP)]
        q_in.append(pltpu.make_async_copy(src, q_packed.at[i - 1], in_sems.at[members + i]))
    d_in = [
        pltpu.make_async_copy(d_refs[i].at[mine[i]], d_buf.at[i], in_sems.at[2 * members + i])
        for i in range(members)
    ]
    gq_out = [pltpu.make_async_copy(gq_buf.at[i], gq_refs[i], out_sems.at[i]) for i in range(members)]
    gk_out = [
        pltpu.make_async_copy(gk_buf.at[i], gk_refs[i], out_sems.at[members + i])
        for i in range(members)
    ]
    for copy in [q_in[0]] + k_in + [d_in[0]] + q_in[1:] + d_in[1:]:
        copy.start()
    whole = part_len * (value // 128)
    for i in range(members):
        k_in[i].wait()
        for pair in range(pairs):
            rest = k_buf[i, pair, CAP * whole : CAP * whole + part_len]
            for j in range(CAP):
                r = i * part + (CAP * pair + j) * part_len
                for lane in range(0, value, 128):
                    c = j * whole + lane // 128 * part_len
                    keys_ref[r : r + part_len, lane : lane + 128] = k_buf[i, pair, c : c + part_len]
                width = latent - value
                keys_ref[r : r + part_len, value:] = rest[:, j * width : (j + 1) * width]
    keys = keys_ref[...]
    nt = (((1,), (1,)), ((), ()))
    shape = (part_len, cols)
    limit = first_ref[0] + lax.broadcasted_iota(jnp.int32, shape, 1) // heads
    limit = limit - lax.broadcasted_iota(jnp.int32, shape, 0)
    def load(tile):
        q_in[tile].wait()
        if tile > 0:
            whole_q = heads * (value // 128)
            for pair in range(rows // CAP):
                rest = q_packed[tile - 1, pair, CAP * whole_q : CAP * whole_q + heads]
                for j in range(CAP):
                    r = CAP * pair + j
                    for lane in range(0, value, 128):
                        c = j * whole_q + lane // 128 * heads
                        q_buf[tile, r, :, lane : lane + 128] = q_packed[tile - 1, pair, c : c + heads]
                    width = latent - value
                    q_buf[tile, r, :, value:] = rest[:, j * width : (j + 1) * width]
        d_in[tile].wait()
        q = q_buf[tile].reshape(cols, latent)
        d = d_buf[tile].reshape(cols, value)
        scores = lax.dot_general(keys, q, nt, preferred_element_type=jnp.float32)
        grad_probs = lax.dot_general(keys[:, :value], d, nt, preferred_element_type=jnp.float32)
        return q, d, scores, grad_probs

    ahead = load(0)
    for tile in range(members):
        q, d, scores, grad_probs = ahead
        strips = []
        for i in range(members * entries):
            strip = scores[i * part_len : (i + 1) * part_len]
            strips.append(jnp.where(start_ref[i] <= limit, strip, -jnp.inf))
        masked = jnp.concatenate(strips, axis=0)
        top = jnp.max(masked, axis=0, keepdims=True)
        expo = jnp.exp2((masked - top) * (SCALE * LOG2E))
        inverse = 1.0 / jnp.sum(expo, axis=0, keepdims=True)
        delta = jnp.sum(expo * grad_probs, axis=0, keepdims=True) * inverse
        probs_low = (expo * inverse).astype(jnp.bfloat16)
        grad_low = (expo * (inverse * SCALE) * (grad_probs - delta)).astype(jnp.bfloat16)
        if tile + 1 < members:
            ahead = load(tile + 1)
        gq = lax.dot_general(
            grad_low, keys, (((0,), (0,)), ((), ())), preferred_element_type=jnp.float32
        )
        gq_buf[tile] = gq.astype(jnp.bfloat16).reshape(rows, heads, latent)
        gq_out[tile].start()
        p_ref[:, tile * cols : (tile + 1) * cols] = probs_low
        g_ref[:, tile * cols : (tile + 1) * cols] = grad_low
    q_all = q_buf[...].reshape(members * cols, latent)
    d_all = d_buf[...].reshape(members * cols, value)
    for i in range(members):
        here = slice(i * part, (i + 1) * part)
        gk = jnp.dot(g_ref[here], q_all, preferred_element_type=jnp.float32)
        gv = jnp.dot(p_ref[here], d_all, preferred_element_type=jnp.float32)
        total = jnp.concatenate([gk[:, :value] + gv, gk[:, value:]], axis=1)
        total = total.astype(jnp.bfloat16)
        for pair in range(pairs):
            r = CAP * pair * part_len
            two = [total[r + j * part_len : r + (j + 1) * part_len] for j in range(CAP)]
            pack_pair(two, gk_buf, (i, pair))
        gk_out[i].start()
    for copy in gq_out + gk_out:
        copy.wait()


def attention(start, first, row, q, d, keys):
    members = len(q)
    pairs, packed, _ = keys[0].shape
    _, heads, value = d[0].shape
    latent = q[0].shape[2]
    rows = CAP * pairs
    keys_n = members * pairs * packed * 128 // latent
    flops = 2 * members * rows * heads * keys_n * (3 * latent + 2 * value)
    smem, hbm = pl.BlockSpec(memory_space=pltpu.SMEM), pl.BlockSpec(memory_space=pltpu.HBM)
    low = jnp.bfloat16
    out = pl.pallas_call(
        functools.partial(attention_kernel, members),
        in_specs=[smem] * 3 + [hbm] * (3 * members),
        out_specs=[hbm] * (2 * members),
        out_shape=[jax.ShapeDtypeStruct((rows, heads, latent), low)] * members
        + [jax.ShapeDtypeStruct(keys[0].shape, low)] * members,
        scratch_shapes=[
            pltpu.VMEM((members, rows, heads, latent), low),
            pltpu.VMEM((members, rows, heads, value), low),
            pltpu.VMEM((members, pairs, packed, 128), low),
            pltpu.VMEM((members, rows, heads, latent), low),
            pltpu.VMEM((members, pairs, packed, 128), low),
            pltpu.VMEM((members - 1, rows // CAP) + q[1].shape[1:], low),
            pltpu.VMEM((keys_n, latent), low),
            pltpu.VMEM((keys_n, members * rows * heads), low),
            pltpu.VMEM((keys_n, members * rows * heads), low),
            pltpu.SemaphoreType.DMA((3 * members,)),
            pltpu.SemaphoreType.DMA((2 * members,)),
        ],
        compiler_params=pltpu.CompilerParams(vmem_limit_bytes=VMEM),
        cost_estimate=pl.CostEstimate(flops=flops, bytes_accessed=8 << 20, transcendentals=1 << 20),
    )(start, first, row, *q, *d, *keys)
    return out[:members], out[members:]


def sum_by_block_kernel(count, index_ref, *refs):
    ins, rest_refs = refs[:count], refs[count:]
    local_ref, slots_ref, table_ref, rest_ref, local_buf, low_ref, sems = rest_refs
    pairs = ins[0].shape[0]
    per, part_len, latent = local_buf.shape
    value = table_ref.shape[2]
    width = latent - value
    whole = part_len * (value // 128)
    table_ref[...] = jnp.zeros_like(table_ref)
    rest_ref[...] = jnp.zeros_like(rest_ref)
    for k in range(count):

        def add(i, carry, k=k):
            rest = ins[k][i, CAP * whole : CAP * whole + part_len].astype(jnp.float32)
            for j in range(CAP):
                at = index_ref[CAP * (k * pairs + i) + j]
                for lane in range(0, value, 128):
                    c = j * whole + lane // 128 * part_len
                    x = ins[k][i, c : c + part_len].astype(jnp.float32)
                    table_ref[at, :, lane : lane + 128] += x
                rest_ref[j, at] += rest
            return carry

        lax.fori_loop(0, pairs, add, 0, unroll=2)
    local_buf[:, :, :value] = table_ref[:per]
    total = rest_ref[0, :per, :, :width]
    for j in range(1, CAP):
        total += rest_ref[j, :per, :, j * width : (j + 1) * width]
    local_buf[:, :, value:] = total
    copies = [pltpu.make_async_copy(local_buf, local_ref, sems.at[0])]
    copies[0].start()
    chunks = sems.shape[0] - 1
    each = slots_ref.shape[0] // chunks
    low_lanes = lax.broadcasted_iota(jnp.int32, (part_len, 128), 1) < width
    for c in range(chunks):

        def pack(i, carry):
            r = 0
            for j in range(CAP):
                for lane in range(0, value, 128):
                    x = table_ref[per + CAP * i + j, :, lane : lane + 128]
                    low_ref[i, r : r + part_len] = x.astype(jnp.bfloat16)
                    r += part_len
            a, b = per + CAP * i, per + CAP * i + 1
            first = rest_ref[0, a] + swap_halves(rest_ref[1, a])
            second = swap_halves(rest_ref[0, b]) + rest_ref[1, b]
            low_ref[i, r : r + part_len] = jnp.where(low_lanes, first, second).astype(jnp.bfloat16)
            return carry

        lax.fori_loop(c * each, (c + 1) * each, pack, 0, unroll=4)
        here = pl.ds(c * each, each)
        copies.append(pltpu.make_async_copy(low_ref.at[here], slots_ref.at[here], sems.at[1 + c]))
        copies[-1].start()
    for copy in copies:
        copy.wait()


def sum_by_block(index, pieces, per_shard, owners, latent):
    packed = pieces[0].shape[1]
    part_len = packed * 128 // (CAP * latent)
    value = latent // 128 * 128
    rows = per_shard + CAP * owners
    vmem = pl.BlockSpec(memory_space=pltpu.VMEM)
    hbm = pl.BlockSpec(memory_space=pltpu.HBM)
    return pl.pallas_call(
        functools.partial(sum_by_block_kernel, len(pieces)),
        in_specs=[pl.BlockSpec(memory_space=pltpu.SMEM)] + [vmem] * len(pieces),
        out_specs=[hbm] * 2,
        out_shape=[
            jax.ShapeDtypeStruct((per_shard, part_len, latent), jnp.float32),
            jax.ShapeDtypeStruct((owners, packed, 128), jnp.bfloat16),
        ],
        scratch_shapes=[
            pltpu.VMEM((rows, part_len, value), jnp.float32),
            pltpu.VMEM((CAP, rows, part_len, 128), jnp.float32),
            pltpu.VMEM((per_shard, part_len, latent), jnp.float32),
            pltpu.VMEM((owners, packed, 128), jnp.bfloat16),
            pltpu.SemaphoreType.DMA((5,)),
        ],
        compiler_params=pltpu.CompilerParams(vmem_limit_bytes=VMEM),
        cost_estimate=pl.CostEstimate(flops=2 << 20, bytes_accessed=6 << 20, transcendentals=0),
    )(index, *pieces)


def receive_kernel(index_ref, in_ref, local_ref, out_ref, table_ref, rest_ref):
    per, part_len, latent = local_ref.shape
    value = (latent // 128) * 128
    rest = latent - value
    last = CAP * part_len * (value // 128)
    table_ref[:per] = local_ref[:, :, :value]
    rest_ref[...] = jnp.zeros_like(rest_ref)

    def add(i, carry):
        for j in range(CAP):
            at = index_ref[CAP * i + j]
            r = j * part_len * (value // 128)
            for lane in range(0, value, 128):
                table_ref[at, :, lane : lane + 128] += in_ref[i, r : r + part_len].astype(jnp.float32)
                r += part_len
            rest_ref[j, at] += in_ref[i, last : last + part_len].astype(jnp.float32)
        return carry

    lax.fori_loop(0, in_ref.shape[0], add, 0, unroll=2)
    out_ref[:, :, :value] = table_ref[:per]
    total = local_ref[:, :, value:]
    for j in range(CAP):
        total += rest_ref[j, :per, :, j * rest : (j + 1) * rest]
    out_ref[:, :, value:] = total


def receive(index, arrived, local):
    per, part_len, latent = local.shape
    return pl.pallas_call(
        receive_kernel,
        in_specs=[
            pl.BlockSpec(memory_space=pltpu.SMEM),
            pl.BlockSpec(memory_space=pltpu.VMEM),
            pl.BlockSpec(memory_space=pltpu.VMEM),
        ],
        out_specs=pl.BlockSpec(memory_space=pltpu.VMEM),
        out_shape=jax.ShapeDtypeStruct(local.shape, jnp.float32),
        scratch_shapes=[
            pltpu.VMEM((per + 1, part_len, latent // 128 * 128), jnp.float32),
            pltpu.VMEM((CAP, per + 1, part_len, 128), jnp.float32),
        ],
        compiler_params=pltpu.CompilerParams(vmem_limit_bytes=12 * 1024 * 1024),
        cost_estimate=pl.CostEstimate(flops=2 << 20, bytes_accessed=4 << 20, transcendentals=0),
    )(index, arrived, local)


def split_kernel(row_ref, in_ref, *refs):
    outs, (buf, sems) = refs[:-2], refs[-2:]
    count, rows = len(outs), outs[0].shape[0]
    ins = [
        pltpu.make_async_copy(in_ref.at[pl.ds(row_ref[k], rows)], buf.at[k], sems.at[k])
        for k in range(count)
    ]
    backs = [pltpu.make_async_copy(buf.at[k], outs[k], sems.at[count + k]) for k in range(count)]
    for copy in ins:
        copy.start()
    for copy, back in zip(ins, backs):
        copy.wait()
        back.start()
    for back in backs:
        back.wait()


def split_rows(row, x, rows):
    count = row.shape[0]
    hbm = pl.BlockSpec(memory_space=pltpu.HBM)
    shape = (rows,) + x.shape[1:]
    return pl.pallas_call(
        split_kernel,
        in_specs=[pl.BlockSpec(memory_space=pltpu.SMEM), hbm],
        out_specs=[hbm] * count,
        out_shape=[jax.ShapeDtypeStruct(shape, x.dtype)] * count,
        scratch_shapes=[
            pltpu.VMEM((count,) + shape, x.dtype),
            pltpu.SemaphoreType.DMA((2 * count,)),
        ],
        compiler_params=pltpu.CompilerParams(vmem_limit_bytes=VMEM),
        cost_estimate=pl.CostEstimate(flops=0, bytes_accessed=4 << 20, transcendentals=0),
    )(row, x)


def split_pack_kernel(row_ref, in_ref, *refs):
    outs, (buf, out_buf, sems) = refs[:-3], refs[-3:]
    count, rows = buf.shape[0], buf.shape[1]
    ins = [
        pltpu.make_async_copy(in_ref.at[pl.ds(row_ref[k], rows)], buf.at[k], sems.at[k])
        for k in range(count)
    ]
    backs = [pltpu.make_async_copy(out_buf.at[k], outs[k], sems.at[count + k]) for k in range(count)]
    for copy in ins:
        copy.start()
    for k in range(count):
        ins[k].wait()

        def move(i, carry, k=k):
            pack_pair([buf[k, CAP * i + j] for j in range(CAP)], out_buf, (k, i))
            return carry

        lax.fori_loop(0, rows // CAP, move, 0, unroll=4)
        backs[k].start()
    for back in backs:
        back.wait()


def split_pack_rows(row, x, rows):
    count = row.shape[0]
    hbm = pl.BlockSpec(memory_space=pltpu.HBM)
    shape = (rows // CAP, CAP * x.shape[1] * x.shape[2] // 128, 128)
    return pl.pallas_call(
        split_pack_kernel,
        in_specs=[pl.BlockSpec(memory_space=pltpu.SMEM), hbm],
        out_specs=[hbm] * count,
        out_shape=[jax.ShapeDtypeStruct(shape, x.dtype)] * count,
        scratch_shapes=[
            pltpu.VMEM((count, rows) + x.shape[1:], x.dtype),
            pltpu.VMEM((count,) + shape, x.dtype),
            pltpu.SemaphoreType.DMA((2 * count,)),
        ],
        compiler_params=pltpu.CompilerParams(vmem_limit_bytes=VMEM),
        cost_estimate=pl.CostEstimate(flops=0, bytes_accessed=4 << 20, transcendentals=0),
    )(row, x)


def join_kernel(row_ref, *refs):
    out_ref = refs[-1]
    for k, ref in enumerate(refs[:-1]):
        out_ref[pl.ds(row_ref[k], ref.shape[0])] = ref[...]


def join_rows(row, pieces):
    rows = sum(p.shape[0] for p in pieces)
    vmem = pl.BlockSpec(memory_space=pltpu.VMEM)
    return pl.pallas_call(
        join_kernel,
        in_specs=[pl.BlockSpec(memory_space=pltpu.SMEM)] + [vmem] * len(pieces),
        out_specs=vmem,
        out_shape=jax.ShapeDtypeStruct((rows,) + pieces[0].shape[1:], pieces[0].dtype),
        compiler_params=pltpu.CompilerParams(vmem_limit_bytes=VMEM),
        cost_estimate=pl.CostEstimate(flops=0, bytes_accessed=5 << 20, transcendentals=0),
    )(row, *pieces)


def ask_kernel(index_ref, line_ref, out_ref, line_buf, out_buf, sems):
    load = pltpu.make_async_copy(line_ref, line_buf, sems.at[0])
    load.start()
    load.wait()

    def move(i, carry):
        pack_pair([line_buf[index_ref[CAP * i + j]] for j in range(CAP)], out_buf, (i,))
        return carry

    chunks = sems.shape[0] - 1
    each = out_ref.shape[0] // chunks
    backs = []
    for c in range(chunks):
        lax.fori_loop(c * each, (c + 1) * each, move, 0, unroll=4)
        here = pl.ds(c * each, each)
        backs.append(pltpu.make_async_copy(out_buf.at[here], out_ref.at[here], sems.at[1 + c]))
        backs[-1].start()
    for back in backs:
        back.wait()


def ask(index, line):
    _, part_len, latent = line.shape
    hbm = pl.BlockSpec(memory_space=pltpu.HBM)
    shape = (index.shape[0] // CAP, CAP * part_len * latent // 128, 128)
    return pl.pallas_call(
        ask_kernel,
        in_specs=[pl.BlockSpec(memory_space=pltpu.SMEM), hbm],
        out_specs=hbm,
        out_shape=jax.ShapeDtypeStruct(shape, line.dtype),
        scratch_shapes=[
            pltpu.VMEM(line.shape, line.dtype),
            pltpu.VMEM(shape, line.dtype),
            pltpu.SemaphoreType.DMA((5,)),
        ],
        compiler_params=pltpu.CompilerParams(vmem_limit_bytes=VMEM // 3),
        cost_estimate=pl.CostEstimate(flops=0, bytes_accessed=4 << 20, transcendentals=0),
    )(index, line)


def pick_kernel(pieces, index_ref, table_ref, own_ref, *refs):
    outs, (table_buf, own_buf, out_buf, in_sems, out_sems) = refs[:pieces], refs[pieces:]
    size, packed = table_ref.shape[0], table_ref.shape[1]
    own, part_len, latent = own_buf.shape
    pairs = out_buf.shape[1]
    whole = part_len * (latent // 128)
    loads = [
        pltpu.make_async_copy(own_ref, own_buf, in_sems.at[0]),
        pltpu.make_async_copy(table_ref, table_buf.at[pl.ds(0, size)], in_sems.at[1]),
    ]
    for load in loads:
        load.start()
    loads[0].wait()
    for i in range(own // CAP):
        pack_pair([own_buf[CAP * i + j] for j in range(CAP)], table_buf, (size + i,))
    loads[1].wait()
    low_lanes = lax.broadcasted_iota(jnp.int32, (part_len, 128), 1) < latent % 128
    backs = []
    for k in range(pieces):

        def move(i, carry, k=k):
            rests = []
            for j in range(CAP):
                e = index_ref[CAP * (k * pairs + i) + j]
                at, side = e // CAP, e % CAP
                src = pl.ds(pl.multiple_of(side * whole, whole), whole)
                out_buf[k, i, j * whole : (j + 1) * whole] = table_buf[at, src]
                rest = table_buf[at, CAP * whole : packed]
                rests.append(jnp.where(side == j, rest, swap_halves(rest)))
            out_buf[k, i, CAP * whole : packed] = jnp.where(low_lanes, rests[0], rests[1])
            return carry

        lax.fori_loop(0, pairs, move, 0, unroll=4)
        backs.append(pltpu.make_async_copy(out_buf.at[k], outs[k], out_sems.at[k]))
        backs[-1].start()
    for back in backs:
        back.wait()


def pick(index, table, own, pieces):
    hbm = pl.BlockSpec(memory_space=pltpu.HBM)
    size, packed, _ = table.shape
    pairs = index.shape[0] // (CAP * pieces)
    return pl.pallas_call(
        functools.partial(pick_kernel, pieces),
        in_specs=[pl.BlockSpec(memory_space=pltpu.SMEM), hbm, hbm],
        out_specs=[hbm] * pieces,
        out_shape=[jax.ShapeDtypeStruct((pairs, packed, 128), table.dtype)] * pieces,
        scratch_shapes=[
            pltpu.VMEM((size + own.shape[0] // CAP, packed, 128), table.dtype),
            pltpu.VMEM(own.shape, own.dtype),
            pltpu.VMEM((pieces, pairs, packed, 128), table.dtype),
            pltpu.SemaphoreType.DMA((2,)),
            pltpu.SemaphoreType.DMA((pieces,)),
        ],
        compiler_params=pltpu.CompilerParams(vmem_limit_bytes=VMEM // 3),
        cost_estimate=pl.CostEstimate(flops=0, bytes_accessed=4 << 20, transcendentals=0),
    )(index, table, own)


def body(query, latent_cache, block_lists, d_out):
    ax, az, ac = lax.axis_index("x"), lax.axis_index("z"), lax.axis_index("core")
    nx, nz, nc = lax.axis_size("x"), lax.axis_size("z"), lax.axis_size("core")
    shards = nx * nz * nc
    shard = (ax * nz + az) * nc + ac
    member = lax.axis_index("vocab")
    members = lax.axis_size("vocab")
    per_shard, block_len, latent = latent_cache.shape
    rows, heads, _ = query.shape
    groups, select = block_lists.shape
    qgroup = rows // groups
    part_len = block_len // members
    groups_mine = groups // members
    slots = shards * CAP
    barrier = lax.optimization_barrier
    ahead = [lax.rem(member + k, members) for k in range(members)]
    behind = [lax.rem(member - k + members, members) for k in range(members)]

    def ring(x, axis, size, k):
        return lax.ppermute(x, axis, [(i, (i + k) % size) for i in range(size)])

    def shift(x, k):
        return x if k % members == 0 else ring(x, "vocab", members, k)

    flat = block_lists.reshape(-1)
    owner = jnp.where(flat >= 0, flat // per_shard, -1)
    local = owner == shard

    def ranks(entries, blocks, cols):
        matches = entries[..., None] == blocks
        present = jnp.any(matches, axis=-2).astype(jnp.int32)
        rank = jnp.cumsum(present.reshape(present.shape[:-1] + (cols, per_shard)), axis=-1)
        return matches, present.reshape(rank.shape), rank

    every_block = jnp.arange(shards * per_shard, dtype=jnp.int32)
    matches, _, rank = ranks(flat, every_block, shards)
    slot_rank = jnp.sum(matches.astype(jnp.int32) * rank.reshape(-1)[None, :], axis=1) - 1
    own_block = flat - shard * per_shard
    table_index = jnp.where(local, own_block, per_shard + owner * CAP + slot_rank)
    table_index = jnp.where(flat >= 0, table_index, 0).reshape(groups, select)
    owner_x, owner_z, owner_c = owner // (nz * nc), owner // nc % nz, owner % nc
    fetch_index = ((owner_x * nc + owner_c) * nz + owner_z) * CAP + slot_rank
    fetch_index = jnp.where(local, slots + own_block, fetch_index)
    fetch_index = jnp.where(flat >= 0, fetch_index, slots).reshape(groups, select)

    peers = nx * nc
    both = jnp.stack([flat, ring(flat, "core", nc, 1)])
    near, hop = both[None], 1
    while hop < nx:
        near = jnp.concatenate([near, ring(near, "x", nx, -hop)])
        hop *= 2
    turn = lax.rem(jnp.arange(nx, dtype=jnp.int32) - ax + nx, nx)
    swap = lax.rem(jnp.arange(nc, dtype=jnp.int32) + ac, nc)
    near = near[turn][:, swap].reshape(peers, groups * select)
    line_owner = (ax * nz + jnp.arange(nz, dtype=jnp.int32)) * nc + ac
    line_block = (line_owner[:, None] * per_shard + jnp.arange(per_shard, dtype=jnp.int32)).reshape(-1)
    _, present, rank = ranks(near, line_block, nz)
    hit = present[:, :, None, :] * (rank[:, :, None, :] == jnp.arange(1, CAP + 1)[:, None])
    block_of = jnp.arange(per_shard, dtype=jnp.int32)
    asked = jnp.sum(hit * block_of, axis=-1) + jnp.sum(hit, axis=-1) - 1

    quarter = lax.dynamic_slice_in_dim(latent_cache, member * part_len, part_len, 1)
    line = lax.all_to_all(jnp.broadcast_to(quarter, (nz,) + quarter.shape), "z", 0, 0, tiled=True)
    line = line.reshape(nz * per_shard, part_len, latent)

    row_ahead = jnp.stack(ahead) * (rows // members)
    d_sent = split_rows(row_ahead[1:], d_out, rows // members)
    d = [d_out] + [shift(d_sent[k - 1], k) for k in range(1, members)]
    q_sent = split_pack_rows(row_ahead[1:], query, rows // members)

    base = jnp.arange(nz, dtype=jnp.int32) * per_shard
    line_index = (base[None, :, None] + jnp.maximum(asked, 0)).reshape(-1)
    line, d[1:], q_sent = barrier((line, d[1:], q_sent))
    q = [query] + [shift(q_sent[k - 1], k) for k in range(1, members)]
    sent = ask(line_index, line)
    table = lax.all_to_all(
        sent.reshape((peers, nz) + sent.shape[1:]), ("x", "core"), 0, 0, tiled=True
    ).reshape(sent.shape)

    first_row = (shard + 1) * (per_shard * block_len) - rows
    part_start = jnp.stack(behind) * part_len
    list_ids = [jnp.stack(ahead) * groups_mine + g for g in range(groups_mine)]
    table, q[1:] = barrier((table, q[1:]))
    keys = []
    for g in range(groups_mine):
        index = fetch_index[list_ids[g]].reshape(-1)
        picked = pick(index, table, quarter, members)
        keys.append([shift(picked[k], k) for k in range(members)])
    grad_q, entries = [], []
    for g in range(groups_mine):
        mine = lax.dynamic_index_in_dim(block_lists, member * groups_mine + g, 0, keepdims=False)
        start = jnp.where(
            mine[None, :] >= 0, mine[None, :] * block_len + part_start[:, None], 1 << 30
        ).reshape(-1)
        first = first_row + (member * groups_mine + g) * qgroup
        row = [member * (rows // members)] + [jnp.int32(0)] * (members - 1)
        row = jnp.stack(row) + g * qgroup
        gq, gk = attention(start, first.reshape(1), row, q, d, keys[g])
        grad_q.append(gq)
        if g < groups_mine - 1:
            gk = [shift(gk[k], -k) for k in range(members)]
        entries += gk
    asked, entries[-members:] = barrier((asked, entries[-members:]))
    incoming = lax.all_to_all(asked.transpose(1, 0, 2), "z", 0, 0, tiled=True)
    incoming = incoming.reshape(nz, nx, nc, CAP).transpose(1, 0, 2, 3).reshape(-1)
    incoming_index = jnp.where(incoming >= 0, incoming, per_shard)
    entries[-members:] = [shift(entries[k - members], -k) for k in range(members)]
    entry_index = jnp.concatenate([table_index[ids].reshape(-1) for ids in list_ids])

    entry_index, incoming_index = barrier((entry_index, incoming_index))
    local_grad, outgoing = sum_by_block(entry_index, entries, per_shard, shards, latent)
    arrived = lax.all_to_all(outgoing, ("x", "z", "core"), 0, 0, tiled=True)
    grad_cache = receive(incoming_index, arrived, local_grad)

    grad_q, _ = barrier((grad_q, outgoing))
    pieces = [shift(grad_q[g][k], -k) for g in range(groups_mine) for k in range(members)]
    place = jnp.concatenate([row_ahead + g * qgroup for g in range(groups_mine)])
    grad_query = join_rows(place, pieces)
    return grad_query, grad_cache


def solution(mesh):
    names = ("x", "z", "core", "vocab")
    mesh = jax.sharding.Mesh(mesh.devices.reshape(4, 8, 2, 4), names)
    seq = names[:3]
    in_specs = (P(seq, "vocab", None), P(seq, None, None), P(seq, None), P(seq, "vocab", None))
    out_specs = (P(seq, "vocab", None), P(seq, "vocab", None))
    return jax.shard_map(body, mesh=mesh, in_specs=in_specs, out_specs=out_specs, check_vma=False)
```

```python
import functools

import jax
import jax.numpy as jnp
from jax import lax
from jax.experimental import pallas as pl
from jax.experimental.pallas import tpu as pltpu
from jax.sharding import PartitionSpec as P

CAP = 2
SCALE = 0.07216878364870323
LOG2E = 1.4426950408889634
VMEM = 60 * 1024 * 1024


def swap_halves(x):
    half = x.shape[1] // 2
    return jnp.concatenate([x[:, half:], x[:, :half]], axis=1)


def pack_pair(two, dst_ref, at):
    tokens, latent = two[0].shape
    value = latent // 128 * 128
    r = 0
    for x in two:
        for lane in range(0, value, 128):
            dst_ref[at + (slice(r, r + tokens),)] = x[:, lane : lane + 128]
            r += tokens
    dst_ref[at + (slice(r, r + tokens),)] = jnp.concatenate([x[:, value:] for x in two], axis=1)


def attention_kernel(members, start_ref, first_ref, row_ref, *refs):
    q_refs, d_refs, k_refs = refs[:members], refs[members : 2 * members], refs[2 * members : 3 * members]
    gq_refs, gk_refs = refs[3 * members : 4 * members], refs[4 * members : 5 * members]
    q_buf, d_buf, k_buf, gq_buf, gk_buf, q_packed, keys_ref, p_ref, g_ref, in_sems, out_sems = refs[5 * members :]
    _, rows, heads, latent = q_buf.shape
    value = d_buf.shape[3]
    pairs, part_len = k_buf.shape[1], k_buf.shape[2] * 128 // (CAP * latent)
    entries = CAP * pairs
    part = entries * part_len
    cols = rows * heads
    mine = [pl.ds(row_ref[i], rows) for i in range(members)]
    k_in = [pltpu.make_async_copy(k_refs[i], k_buf.at[i], in_sems.at[i]) for i in range(members)]
    q_in = [pltpu.make_async_copy(q_refs[0].at[mine[0]], q_buf.at[0], in_sems.at[members])]
    for i in range(1, members):
        src = q_refs[i].at[pl.ds(row_ref[i] // CAP, rows // CAP)]
        q_in.append(pltpu.make_async_copy(src, q_packed.at[i - 1], in_sems.at[members + i]))
    d_in = [
        pltpu.make_async_copy(d_refs[i].at[mine[i]], d_buf.at[i], in_sems.at[2 * members + i])
        for i in range(members)
    ]
    gq_out = [pltpu.make_async_copy(gq_buf.at[i], gq_refs[i], out_sems.at[i]) for i in range(members)]
    gk_out = [
        pltpu.make_async_copy(gk_buf.at[i], gk_refs[i], out_sems.at[members + i])
        for i in range(members)
    ]
    for copy in [q_in[0]] + k_in + [d_in[0]] + q_in[1:] + d_in[1:]:
        copy.start()
    whole = part_len * (value // 128)
    for i in range(members):
        k_in[i].wait()
        for pair in range(pairs):
            rest = k_buf[i, pair, CAP * whole : CAP * whole + part_len]
            for j in range(CAP):
                r = i * part + (CAP * pair + j) * part_len
                for lane in range(0, value, 128):
                    c = j * whole + lane // 128 * part_len
                    keys_ref[r : r + part_len, lane : lane + 128] = k_buf[i, pair, c : c + part_len]
                width = latent - value
                keys_ref[r : r + part_len, value:] = rest[:, j * width : (j + 1) * width]
    keys = keys_ref[...]
    nt = (((1,), (1,)), ((), ()))
    shape = (part_len, 2 * cols)
    limit = first_ref[0] + lax.broadcasted_iota(jnp.int32, shape, 1) % cols // heads
    limit = limit - lax.broadcasted_iota(jnp.int32, shape, 0)
    def bring(tile):
        q_in[tile].wait()
        if tile > 0:
            whole_q = heads * (value // 128)
            for pair in range(rows // CAP):
                rest = q_packed[tile - 1, pair, CAP * whole_q : CAP * whole_q + heads]
                for j in range(CAP):
                    r = CAP * pair + j
                    for lane in range(0, value, 128):
                        c = j * whole_q + lane // 128 * heads
                        q_buf[tile, r, :, lane : lane + 128] = q_packed[tile - 1, pair, c : c + heads]
                    width = latent - value
                    q_buf[tile, r, :, value:] = rest[:, j * width : (j + 1) * width]
        d_in[tile].wait()

    span = 2
    wide = span * cols

    def load(step):
        for tile in range(step * span, (step + 1) * span):
            bring(tile)
        q = q_buf[step * span : (step + 1) * span].reshape(wide, latent)
        d = d_buf[step * span : (step + 1) * span].reshape(wide, value)
        scores = lax.dot_general(keys, q, nt, preferred_element_type=jnp.float32)
        grad_probs = lax.dot_general(keys[:, :value], d, nt, preferred_element_type=jnp.float32)
        return scores, grad_probs

    ahead = load(0)
    for step in range(members // span):
        scores, grad_probs = ahead
        strips = []
        for i in range(members * entries):
            strip = scores[i * part_len : (i + 1) * part_len]
            strips.append(jnp.where(start_ref[i] <= limit, strip, -jnp.inf))
        masked = jnp.concatenate(strips, axis=0)
        top = jnp.max(masked, axis=0, keepdims=True)
        expo = jnp.exp2((masked - top) * (SCALE * LOG2E))
        inverse = 1.0 / jnp.sum(expo, axis=0, keepdims=True)
        delta = jnp.sum(expo * grad_probs, axis=0, keepdims=True) * inverse
        probs_low = (expo * inverse).astype(jnp.bfloat16)
        grad_low = (expo * (inverse * SCALE) * (grad_probs - delta)).astype(jnp.bfloat16)
        if (step + 1) * span < members:
            ahead = load(step + 1)
        gq = lax.dot_general(
            grad_low, keys, (((0,), (0,)), ((), ())), preferred_element_type=jnp.float32
        )
        gq = gq.astype(jnp.bfloat16).reshape(span, rows, heads, latent)
        for j in range(span):
            gq_buf[step * span + j] = gq[j]
            gq_out[step * span + j].start()
        p_ref[:, step * wide : (step + 1) * wide] = probs_low
        g_ref[:, step * wide : (step + 1) * wide] = grad_low
    q_all = q_buf[...].reshape(members * cols, latent)
    d_all = d_buf[...].reshape(members * cols, value)
    for i in range(members):
        here = slice(i * part, (i + 1) * part)
        gk = jnp.dot(g_ref[here], q_all, preferred_element_type=jnp.float32)
        gv = jnp.dot(p_ref[here], d_all, preferred_element_type=jnp.float32)
        total = jnp.concatenate([gk[:, :value] + gv, gk[:, value:]], axis=1)
        total = total.astype(jnp.bfloat16)
        for pair in range(pairs):
            r = CAP * pair * part_len
            two = [total[r + j * part_len : r + (j + 1) * part_len] for j in range(CAP)]
            pack_pair(two, gk_buf, (i, pair))
        gk_out[i].start()
    for copy in gq_out + gk_out:
        copy.wait()


def attention(start, first, row, q, d, keys):
    members = len(q)
    pairs, packed, _ = keys[0].shape
    _, heads, value = d[0].shape
    latent = q[0].shape[2]
    rows = CAP * pairs
    keys_n = members * pairs * packed * 128 // latent
    flops = 2 * members * rows * heads * keys_n * (3 * latent + 2 * value)
    smem, hbm = pl.BlockSpec(memory_space=pltpu.SMEM), pl.BlockSpec(memory_space=pltpu.HBM)
    low = jnp.bfloat16
    out = pl.pallas_call(
        functools.partial(attention_kernel, members),
        in_specs=[smem] * 3 + [hbm] * (3 * members),
        out_specs=[hbm] * (2 * members),
        out_shape=[jax.ShapeDtypeStruct((rows, heads, latent), low)] * members
        + [jax.ShapeDtypeStruct(keys[0].shape, low)] * members,
        scratch_shapes=[
            pltpu.VMEM((members, rows, heads, latent), low),
            pltpu.VMEM((members, rows, heads, value), low),
            pltpu.VMEM((members, pairs, packed, 128), low),
            pltpu.VMEM((members, rows, heads, latent), low),
            pltpu.VMEM((members, pairs, packed, 128), low),
            pltpu.VMEM((members - 1, rows // CAP) + q[1].shape[1:], low),
            pltpu.VMEM((keys_n, latent), low),
            pltpu.VMEM((keys_n, members * rows * heads), low),
            pltpu.VMEM((keys_n, members * rows * heads), low),
            pltpu.SemaphoreType.DMA((3 * members,)),
            pltpu.SemaphoreType.DMA((2 * members,)),
        ],
        compiler_params=pltpu.CompilerParams(vmem_limit_bytes=VMEM),
        cost_estimate=pl.CostEstimate(flops=flops, bytes_accessed=8 << 20, transcendentals=1 << 20),
    )(start, first, row, *q, *d, *keys)
    return out[:members], out[members:]


def sum_by_block_kernel(count, index_ref, *refs):
    ins, rest_refs = refs[:count], refs[count:]
    local_ref, slots_ref, table_ref, rest_ref, local_buf, low_ref, sems = rest_refs
    pairs = ins[0].shape[0]
    per, part_len, latent = local_buf.shape
    value = table_ref.shape[2]
    width = latent - value
    whole = part_len * (value // 128)
    table_ref[...] = jnp.zeros_like(table_ref)
    rest_ref[...] = jnp.zeros_like(rest_ref)
    for k in range(count):

        def add(i, carry, k=k):
            rest = ins[k][i, CAP * whole : CAP * whole + part_len].astype(jnp.float32)
            for j in range(CAP):
                at = index_ref[CAP * (k * pairs + i) + j]
                for lane in range(0, value, 128):
                    c = j * whole + lane // 128 * part_len
                    x = ins[k][i, c : c + part_len].astype(jnp.float32)
                    table_ref[at, :, lane : lane + 128] += x
                rest_ref[j, at] += rest
            return carry

        lax.fori_loop(0, pairs, add, 0, unroll=2)
    local_buf[:, :, :value] = table_ref[:per]
    total = rest_ref[0, :per, :, :width]
    for j in range(1, CAP):
        total += rest_ref[j, :per, :, j * width : (j + 1) * width]
    local_buf[:, :, value:] = total
    copies = [pltpu.make_async_copy(local_buf, local_ref, sems.at[0])]
    copies[0].start()
    chunks = sems.shape[0] - 1
    each = slots_ref.shape[0] // chunks
    low_lanes = lax.broadcasted_iota(jnp.int32, (part_len, 128), 1) < width
    for c in range(chunks):

        def pack(i, carry):
            r = 0
            for j in range(CAP):
                for lane in range(0, value, 128):
                    x = table_ref[per + CAP * i + j, :, lane : lane + 128]
                    low_ref[i, r : r + part_len] = x.astype(jnp.bfloat16)
                    r += part_len
            a, b = per + CAP * i, per + CAP * i + 1
            first = rest_ref[0, a] + swap_halves(rest_ref[1, a])
            second = swap_halves(rest_ref[0, b]) + rest_ref[1, b]
            low_ref[i, r : r + part_len] = jnp.where(low_lanes, first, second).astype(jnp.bfloat16)
            return carry

        lax.fori_loop(c * each, (c + 1) * each, pack, 0, unroll=4)
        here = pl.ds(c * each, each)
        copies.append(pltpu.make_async_copy(low_ref.at[here], slots_ref.at[here], sems.at[1 + c]))
        copies[-1].start()
    for copy in copies:
        copy.wait()


def sum_by_block(index, pieces, per_shard, owners, latent):
    packed = pieces[0].shape[1]
    part_len = packed * 128 // (CAP * latent)
    value = latent // 128 * 128
    rows = per_shard + CAP * owners
    vmem = pl.BlockSpec(memory_space=pltpu.VMEM)
    hbm = pl.BlockSpec(memory_space=pltpu.HBM)
    return pl.pallas_call(
        functools.partial(sum_by_block_kernel, len(pieces)),
        in_specs=[pl.BlockSpec(memory_space=pltpu.SMEM)] + [vmem] * len(pieces),
        out_specs=[hbm] * 2,
        out_shape=[
            jax.ShapeDtypeStruct((per_shard, part_len, latent), jnp.float32),
            jax.ShapeDtypeStruct((owners, packed, 128), jnp.bfloat16),
        ],
        scratch_shapes=[
            pltpu.VMEM((rows, part_len, value), jnp.float32),
            pltpu.VMEM((CAP, rows, part_len, 128), jnp.float32),
            pltpu.VMEM((per_shard, part_len, latent), jnp.float32),
            pltpu.VMEM((owners, packed, 128), jnp.bfloat16),
            pltpu.SemaphoreType.DMA((5,)),
        ],
        compiler_params=pltpu.CompilerParams(vmem_limit_bytes=VMEM),
        cost_estimate=pl.CostEstimate(flops=2 << 20, bytes_accessed=6 << 20, transcendentals=0),
    )(index, *pieces)


def receive_kernel(index_ref, in_ref, local_ref, out_ref, table_ref, rest_ref):
    per, part_len, latent = local_ref.shape
    value = (latent // 128) * 128
    rest = latent - value
    last = CAP * part_len * (value // 128)
    table_ref[:per] = local_ref[:, :, :value]
    rest_ref[...] = jnp.zeros_like(rest_ref)

    def add(i, carry):
        for j in range(CAP):
            at = index_ref[CAP * i + j]
            r = j * part_len * (value // 128)
            for lane in range(0, value, 128):
                table_ref[at, :, lane : lane + 128] += in_ref[i, r : r + part_len].astype(jnp.float32)
                r += part_len
            rest_ref[j, at] += in_ref[i, last : last + part_len].astype(jnp.float32)
        return carry

    lax.fori_loop(0, in_ref.shape[0], add, 0, unroll=2)
    out_ref[:, :, :value] = table_ref[:per]
    total = local_ref[:, :, value:]
    for j in range(CAP):
        total += rest_ref[j, :per, :, j * rest : (j + 1) * rest]
    out_ref[:, :, value:] = total


def receive(index, arrived, local):
    per, part_len, latent = local.shape
    return pl.pallas_call(
        receive_kernel,
        in_specs=[
            pl.BlockSpec(memory_space=pltpu.SMEM),
            pl.BlockSpec(memory_space=pltpu.VMEM),
            pl.BlockSpec(memory_space=pltpu.VMEM),
        ],
        out_specs=pl.BlockSpec(memory_space=pltpu.VMEM),
        out_shape=jax.ShapeDtypeStruct(local.shape, jnp.float32),
        scratch_shapes=[
            pltpu.VMEM((per + 1, part_len, latent // 128 * 128), jnp.float32),
            pltpu.VMEM((CAP, per + 1, part_len, 128), jnp.float32),
        ],
        compiler_params=pltpu.CompilerParams(vmem_limit_bytes=12 * 1024 * 1024),
        cost_estimate=pl.CostEstimate(flops=2 << 20, bytes_accessed=4 << 20, transcendentals=0),
    )(index, arrived, local)


def split_kernel(row_ref, in_ref, *refs):
    outs, (buf, sems) = refs[:-2], refs[-2:]
    count, rows = len(outs), outs[0].shape[0]
    ins = [
        pltpu.make_async_copy(in_ref.at[pl.ds(row_ref[k], rows)], buf.at[k], sems.at[k])
        for k in range(count)
    ]
    backs = [pltpu.make_async_copy(buf.at[k], outs[k], sems.at[count + k]) for k in range(count)]
    for copy in ins:
        copy.start()
    for copy, back in zip(ins, backs):
        copy.wait()
        back.start()
    for back in backs:
        back.wait()


def split_rows(row, x, rows):
    count = row.shape[0]
    hbm = pl.BlockSpec(memory_space=pltpu.HBM)
    shape = (rows,) + x.shape[1:]
    return pl.pallas_call(
        split_kernel,
        in_specs=[pl.BlockSpec(memory_space=pltpu.SMEM), hbm],
        out_specs=[hbm] * count,
        out_shape=[jax.ShapeDtypeStruct(shape, x.dtype)] * count,
        scratch_shapes=[
            pltpu.VMEM((count,) + shape, x.dtype),
            pltpu.SemaphoreType.DMA((2 * count,)),
        ],
        compiler_params=pltpu.CompilerParams(vmem_limit_bytes=VMEM),
        cost_estimate=pl.CostEstimate(flops=0, bytes_accessed=4 << 20, transcendentals=0),
    )(row, x)


def split_pack_kernel(row_ref, in_ref, *refs):
    outs, (buf, out_buf, sems) = refs[:-3], refs[-3:]
    count, rows = buf.shape[0], buf.shape[1]
    ins = [
        pltpu.make_async_copy(in_ref.at[pl.ds(row_ref[k], rows)], buf.at[k], sems.at[k])
        for k in range(count)
    ]
    backs = [pltpu.make_async_copy(out_buf.at[k], outs[k], sems.at[count + k]) for k in range(count)]
    for copy in ins:
        copy.start()
    for k in range(count):
        ins[k].wait()

        def move(i, carry, k=k):
            pack_pair([buf[k, CAP * i + j] for j in range(CAP)], out_buf, (k, i))
            return carry

        lax.fori_loop(0, rows // CAP, move, 0, unroll=4)
        backs[k].start()
    for back in backs:
        back.wait()


def split_pack_rows(row, x, rows):
    count = row.shape[0]
    hbm = pl.BlockSpec(memory_space=pltpu.HBM)
    shape = (rows // CAP, CAP * x.shape[1] * x.shape[2] // 128, 128)
    return pl.pallas_call(
        split_pack_kernel,
        in_specs=[pl.BlockSpec(memory_space=pltpu.SMEM), hbm],
        out_specs=[hbm] * count,
        out_shape=[jax.ShapeDtypeStruct(shape, x.dtype)] * count,
        scratch_shapes=[
            pltpu.VMEM((count, rows) + x.shape[1:], x.dtype),
            pltpu.VMEM((count,) + shape, x.dtype),
            pltpu.SemaphoreType.DMA((2 * count,)),
        ],
        compiler_params=pltpu.CompilerParams(vmem_limit_bytes=VMEM),
        cost_estimate=pl.CostEstimate(flops=0, bytes_accessed=4 << 20, transcendentals=0),
    )(row, x)


def join_kernel(row_ref, *refs):
    out_ref = refs[-1]
    for k, ref in enumerate(refs[:-1]):
        out_ref[pl.ds(row_ref[k], ref.shape[0])] = ref[...]


def join_rows(row, pieces):
    rows = sum(p.shape[0] for p in pieces)
    vmem = pl.BlockSpec(memory_space=pltpu.VMEM)
    return pl.pallas_call(
        join_kernel,
        in_specs=[pl.BlockSpec(memory_space=pltpu.SMEM)] + [vmem] * len(pieces),
        out_specs=vmem,
        out_shape=jax.ShapeDtypeStruct((rows,) + pieces[0].shape[1:], pieces[0].dtype),
        compiler_params=pltpu.CompilerParams(vmem_limit_bytes=VMEM),
        cost_estimate=pl.CostEstimate(flops=0, bytes_accessed=5 << 20, transcendentals=0),
    )(row, *pieces)


def ask_kernel(index_ref, line_ref, out_ref, line_buf, out_buf, sems):
    load = pltpu.make_async_copy(line_ref, line_buf, sems.at[0])
    load.start()
    load.wait()

    def move(i, carry):
        pack_pair([line_buf[index_ref[CAP * i + j]] for j in range(CAP)], out_buf, (i,))
        return carry

    chunks = sems.shape[0] - 1
    each = out_ref.shape[0] // chunks
    backs = []
    for c in range(chunks):
        lax.fori_loop(c * each, (c + 1) * each, move, 0, unroll=4)
        here = pl.ds(c * each, each)
        backs.append(pltpu.make_async_copy(out_buf.at[here], out_ref.at[here], sems.at[1 + c]))
        backs[-1].start()
    for back in backs:
        back.wait()


def ask(index, line):
    _, part_len, latent = line.shape
    hbm = pl.BlockSpec(memory_space=pltpu.HBM)
    shape = (index.shape[0] // CAP, CAP * part_len * latent // 128, 128)
    return pl.pallas_call(
        ask_kernel,
        in_specs=[pl.BlockSpec(memory_space=pltpu.SMEM), hbm],
        out_specs=hbm,
        out_shape=jax.ShapeDtypeStruct(shape, line.dtype),
        scratch_shapes=[
            pltpu.VMEM(line.shape, line.dtype),
            pltpu.VMEM(shape, line.dtype),
            pltpu.SemaphoreType.DMA((5,)),
        ],
        compiler_params=pltpu.CompilerParams(vmem_limit_bytes=VMEM // 3),
        cost_estimate=pl.CostEstimate(flops=0, bytes_accessed=4 << 20, transcendentals=0),
    )(index, line)


def pick_kernel(pieces, index_ref, table_ref, own_ref, *refs):
    outs, (table_buf, own_buf, out_buf, in_sems, out_sems) = refs[:pieces], refs[pieces:]
    size, packed = table_ref.shape[0], table_ref.shape[1]
    own, part_len, latent = own_buf.shape
    pairs = out_buf.shape[1]
    whole = part_len * (latent // 128)
    loads = [
        pltpu.make_async_copy(own_ref, own_buf, in_sems.at[0]),
        pltpu.make_async_copy(table_ref, table_buf.at[pl.ds(0, size)], in_sems.at[1]),
    ]
    for load in loads:
        load.start()
    loads[0].wait()
    for i in range(own // CAP):
        pack_pair([own_buf[CAP * i + j] for j in range(CAP)], table_buf, (size + i,))
    loads[1].wait()
    low_lanes = lax.broadcasted_iota(jnp.int32, (part_len, 128), 1) < latent % 128
    backs = []
    for k in range(pieces):

        def move(i, carry, k=k):
            rests = []
            for j in range(CAP):
                e = index_ref[CAP * (k * pairs + i) + j]
                at, side = e // CAP, e % CAP
                src = pl.ds(pl.multiple_of(side * whole, whole), whole)
                out_buf[k, i, j * whole : (j + 1) * whole] = table_buf[at, src]
                rest = table_buf[at, CAP * whole : packed]
                rests.append(jnp.where(side == j, rest, swap_halves(rest)))
            out_buf[k, i, CAP * whole : packed] = jnp.where(low_lanes, rests[0], rests[1])
            return carry

        lax.fori_loop(0, pairs, move, 0, unroll=4)
        backs.append(pltpu.make_async_copy(out_buf.at[k], outs[k], out_sems.at[k]))
        backs[-1].start()
    for back in backs:
        back.wait()


def pick(index, table, own, pieces):
    hbm = pl.BlockSpec(memory_space=pltpu.HBM)
    size, packed, _ = table.shape
    pairs = index.shape[0] // (CAP * pieces)
    return pl.pallas_call(
        functools.partial(pick_kernel, pieces),
        in_specs=[pl.BlockSpec(memory_space=pltpu.SMEM), hbm, hbm],
        out_specs=[hbm] * pieces,
        out_shape=[jax.ShapeDtypeStruct((pairs, packed, 128), table.dtype)] * pieces,
        scratch_shapes=[
            pltpu.VMEM((size + own.shape[0] // CAP, packed, 128), table.dtype),
            pltpu.VMEM(own.shape, own.dtype),
            pltpu.VMEM((pieces, pairs, packed, 128), table.dtype),
            pltpu.SemaphoreType.DMA((2,)),
            pltpu.SemaphoreType.DMA((pieces,)),
        ],
        compiler_params=pltpu.CompilerParams(vmem_limit_bytes=VMEM // 3),
        cost_estimate=pl.CostEstimate(flops=0, bytes_accessed=4 << 20, transcendentals=0),
    )(index, table, own)


def body(query, latent_cache, block_lists, d_out):
    ax, az, ac = lax.axis_index("x"), lax.axis_index("z"), lax.axis_index("core")
    nx, nz, nc = lax.axis_size("x"), lax.axis_size("z"), lax.axis_size("core")
    shards = nx * nz * nc
    shard = (ax * nz + az) * nc + ac
    member = lax.axis_index("vocab")
    members = lax.axis_size("vocab")
    per_shard, block_len, latent = latent_cache.shape
    rows, heads, _ = query.shape
    groups, select = block_lists.shape
    qgroup = rows // groups
    part_len = block_len // members
    groups_mine = groups // members
    slots = shards * CAP
    barrier = lax.optimization_barrier
    ahead = [lax.rem(member + k, members) for k in range(members)]
    behind = [lax.rem(member - k + members, members) for k in range(members)]

    def ring(x, axis, size, k):
        return lax.ppermute(x, axis, [(i, (i + k) % size) for i in range(size)])

    def shift(x, k):
        return x if k % members == 0 else ring(x, "vocab", members, k)

    flat = block_lists.reshape(-1)
    owner = jnp.where(flat >= 0, flat // per_shard, -1)
    local = owner == shard

    def ranks(entries, blocks, cols):
        matches = entries[..., None] == blocks
        present = jnp.any(matches, axis=-2).astype(jnp.int32)
        rank = jnp.cumsum(present.reshape(present.shape[:-1] + (cols, per_shard)), axis=-1)
        return matches, present.reshape(rank.shape), rank

    every_block = jnp.arange(shards * per_shard, dtype=jnp.int32)
    matches, _, rank = ranks(flat, every_block, shards)
    slot_rank = jnp.sum(matches.astype(jnp.int32) * rank.reshape(-1)[None, :], axis=1) - 1
    own_block = flat - shard * per_shard
    table_index = jnp.where(local, own_block, per_shard + owner * CAP + slot_rank)
    table_index = jnp.where(flat >= 0, table_index, 0).reshape(groups, select)
    owner_x, owner_z, owner_c = owner // (nz * nc), owner // nc % nz, owner % nc
    fetch_index = ((owner_x * nc + owner_c) * nz + owner_z) * CAP + slot_rank
    fetch_index = jnp.where(local, slots + own_block, fetch_index)
    fetch_index = jnp.where(flat >= 0, fetch_index, slots).reshape(groups, select)

    peers = nx * nc
    both = jnp.stack([flat, ring(flat, "core", nc, 1)])
    near, hop = both[None], 1
    while hop < nx:
        near = jnp.concatenate([near, ring(near, "x", nx, -hop)])
        hop *= 2
    turn = lax.rem(jnp.arange(nx, dtype=jnp.int32) - ax + nx, nx)
    swap = lax.rem(jnp.arange(nc, dtype=jnp.int32) + ac, nc)
    near = near[turn][:, swap].reshape(peers, groups * select)
    line_owner = (ax * nz + jnp.arange(nz, dtype=jnp.int32)) * nc + ac
    line_block = (line_owner[:, None] * per_shard + jnp.arange(per_shard, dtype=jnp.int32)).reshape(-1)
    _, present, rank = ranks(near, line_block, nz)
    hit = present[:, :, None, :] * (rank[:, :, None, :] == jnp.arange(1, CAP + 1)[:, None])
    block_of = jnp.arange(per_shard, dtype=jnp.int32)
    asked = jnp.sum(hit * block_of, axis=-1) + jnp.sum(hit, axis=-1) - 1

    quarter = lax.dynamic_slice_in_dim(latent_cache, member * part_len, part_len, 1)
    line = lax.all_to_all(jnp.broadcast_to(quarter, (nz,) + quarter.shape), "z", 0, 0, tiled=True)
    line = line.reshape(nz * per_shard, part_len, latent)

    row_ahead = jnp.stack(ahead) * (rows // members)
    d_sent = split_rows(row_ahead[1:], d_out, rows // members)
    d = [d_out] + [shift(d_sent[k - 1], k) for k in range(1, members)]
    q_sent = split_pack_rows(row_ahead[1:], query, rows // members)

    base = jnp.arange(nz, dtype=jnp.int32) * per_shard
    line_index = (base[None, :, None] + jnp.maximum(asked, 0)).reshape(-1)
    line, d[1:], q_sent = barrier((line, d[1:], q_sent))
    q = [query] + [shift(q_sent[k - 1], k) for k in range(1, members)]
    sent = ask(line_index, line)
    table = lax.all_to_all(
        sent.reshape((peers, nz) + sent.shape[1:]), ("x", "core"), 0, 0, tiled=True
    ).reshape(sent.shape)

    first_row = (shard + 1) * (per_shard * block_len) - rows
    part_start = jnp.stack(behind) * part_len
    list_ids = [jnp.stack(ahead) * groups_mine + g for g in range(groups_mine)]
    table, q[1:] = barrier((table, q[1:]))
    keys = []
    for g in range(groups_mine):
        index = fetch_index[list_ids[g]].reshape(-1)
        picked = pick(index, table, quarter, members)
        keys.append([shift(picked[k], k) for k in range(members)])
    grad_q, entries = [], []
    for g in range(groups_mine):
        mine = lax.dynamic_index_in_dim(block_lists, member * groups_mine + g, 0, keepdims=False)
        start = jnp.where(
            mine[None, :] >= 0, mine[None, :] * block_len + part_start[:, None], 1 << 30
        ).reshape(-1)
        first = first_row + (member * groups_mine + g) * qgroup
        row = [member * (rows // members)] + [jnp.int32(0)] * (members - 1)
        row = jnp.stack(row) + g * qgroup
        gq, gk = attention(start, first.reshape(1), row, q, d, keys[g])
        grad_q.append(gq)
        if g < groups_mine - 1:
            gk = [shift(gk[k], -k) for k in range(members)]
        entries += gk
    asked, entries[-members:] = barrier((asked, entries[-members:]))
    incoming = lax.all_to_all(asked.transpose(1, 0, 2), "z", 0, 0, tiled=True)
    incoming = incoming.reshape(nz, nx, nc, CAP).transpose(1, 0, 2, 3).reshape(-1)
    incoming_index = jnp.where(incoming >= 0, incoming, per_shard)
    entries[-members:] = [shift(entries[k - members], -k) for k in range(members)]
    entry_index = jnp.concatenate([table_index[ids].reshape(-1) for ids in list_ids])

    entry_index, incoming_index = barrier((entry_index, incoming_index))
    local_grad, outgoing = sum_by_block(entry_index, entries, per_shard, shards, latent)
    arrived = lax.all_to_all(outgoing, ("x", "z", "core"), 0, 0, tiled=True)
    grad_cache = receive(incoming_index, arrived, local_grad)

    grad_q, _ = barrier((grad_q, outgoing))
    pieces = [shift(grad_q[g][k], -k) for g in range(groups_mine) for k in range(members)]
    place = jnp.concatenate([row_ahead + g * qgroup for g in range(groups_mine)])
    grad_query = join_rows(place, pieces)
    return grad_query, grad_cache


def solution(mesh):
    names = ("x", "z", "core", "vocab")
    mesh = jax.sharding.Mesh(mesh.devices.reshape(4, 8, 2, 4), names)
    seq = names[:3]
    in_specs = (P(seq, "vocab", None), P(seq, None, None), P(seq, None), P(seq, "vocab", None))
    out_specs = (P(seq, "vocab", None), P(seq, "vocab", None))
    return jax.shard_map(body, mesh=mesh, in_specs=in_specs, out_specs=out_specs, check_vma=False)
```
